256 devices in a mesh: seq: 64 (over y, z, core), tp: 4 (over x).
Axes of the slice: x: 4, y: 4, z: 8, core: 2. Of those that a mesh axis runs over, the one named last changes fastest.
Arguments:
- head_input: bfloat16 [49152, 8192], P('seq', 'tp'), may hold values from -6 to 6
- gate_input: bfloat16 [49152, 8192], P('seq', 'tp'), may hold values from -16 to 16
- step_size: float32 [49152, 64], P('seq', 'tp'), may hold values from 0.01 to 0.04
- input_proj: bfloat16 [49152, 128], P('seq'), may hold values from -6 to 6
- output_proj: bfloat16 [49152, 128], P('seq'), may hold values from -6 to 6
- decay_rate: float32 [64], P('tp'), may hold values from 0.0009765625 to 2, as said below
- skip_gain: float32 [64], P('tp'), may hold values from 0.5 to 1.5
- norm_gain: float32 [8192], P('tp'), may hold values from 0.5 to 1.5
- doc_lengths: int32 [16], replicated, may hold values from 1 to 12288, 49152 in all
Outputs:
- mixed_out: bfloat16 [49152, 8192], P('seq', 'tp')
- group_states: float32 [192, 64, 128, 128], P('seq', 'tp')
The draws below stay inside these ranges and needn't reach their ends.
Inputs may be any that keep to these rules, and one draw needn't show every extreme that they name: `doc_lengths`: the lengths sum to 49152; the longest is exactly 12288. `decay_rate`: positive rates.
All inputs are finite; a program needn't handle non-finite values.
Results may differ from the reference program's by a relative error of at most 0.0056.
Values sent between devices are 32-bit elements; how exact they have to be, the bound alone decides.
No kernel may reach another device: no remote copies, remote signals or barrier semaphores. Data moves between devices by JAX's collectives and lax.ppermute only.
A program may use at most 192 MiB of HBM per device.

```python
import math
import jax
import jax.numpy as jnp
import numpy as np
from jax import lax

H = 64
P_SIZE = 128
N = 128
Q = 256
TOKENS = 49152
INNER = 8192
DOCS = 16


def draw_gate_input(key, part):
    key = jax.random.fold_in(key, 11)
    key_base, key_rough = jax.random.split(key)
    position = jnp.arange(INNER, dtype=jnp.float32) / INNER
    column_scale = jnp.exp(math.log(3.0) * position) * jax.random.uniform(key_rough, (INNER,), jnp.float32, 0.7, 1.3)
    base_values = jnp.clip(jax.random.normal(key_base, (TOKENS, INNER), jnp.float32), -4.0, 4.0)
    return (base_values * column_scale[None, :]).astype(jnp.bfloat16)


def draw_decay_rate(key, part):
    key = jax.random.fold_in(key, 12)
    key_pick, key_slow, key_fast = jax.random.split(key, 3)
    fast_share = 0.5
    fast_pick = jax.random.uniform(key_pick, (H,), jnp.float32) < fast_share
    slow_rate = jnp.exp(jax.random.uniform(key_slow, (H,), jnp.float32, math.log(0.3), 0.0)) / (0.025 * (TOKENS // 4))
    fast_rate = jnp.exp(jax.random.uniform(key_fast, (H,), jnp.float32, math.log(0.7), math.log(2.0)))
    return jnp.where(fast_pick, fast_rate, slow_rate).astype(jnp.float32)


def block_levels(rng, shape, cuts, smallest, largest):
    level = 1.0
    for dim, shards_of in cuts:
        heights = jax.random.uniform(jax.random.fold_in(jax.random.fold_in(rng, 6), dim), (shards_of,), jnp.float32, smallest / len(cuts), largest / len(cuts))
        level = level * jnp.repeat(jnp.exp(heights), shape[dim] // shards_of).reshape((-1,) + (1,) * (len(shape) - 1 - dim))
    return level


def split_up(number_of, total, reach, skew):
    portions = [(1 << 20) // math.isqrt(standing ** skew) + 1 for standing in range(2, number_of + 1)]
    spare, counts = total - reach - (number_of - 1), [1] * (number_of - 1)
    while spare > 0:
        candidates = [i for i in range(number_of - 1) if counts[i] < reach]
        whole, budget = sum([portions[i] for i in candidates]), spare
        for i in candidates:
            extra = min(reach - counts[i], max(1, budget * portions[i] // whole), spare)
            counts[i] = counts[i] + extra
            spare = spare - extra
    return np.array([reach] + counts)


def uneven_parts(rng, number_of, total, most, lean):
    if number_of == 2:
        one = jax.random.randint(rng, (), max(1, total - most), min(most, total - 1) + 1)
        return jnp.stack([one, total - one])
    tallies = jnp.asarray(split_up(number_of, total, most, lean), jnp.int32)
    pairs = (number_of - 1) // 2
    donor, receiver = tallies[1:1 + 2 * pairs:2], tallies[2:2 + 2 * pairs:2]
    room = jnp.minimum(donor - 1, most - receiver)
    shifted = jax.random.randint(jax.random.fold_in(rng, 1), (pairs,), 0, 1 << 20) % (room + 1)
    tallies = tallies.at[1:1 + 2 * pairs:2].set(donor - shifted).at[2:2 + 2 * pairs:2].set(receiver + shifted)
    return tallies[jax.random.permutation(jax.random.fold_in(rng, 2), number_of)]


def normal_values(rng, extent, width, bound, cuts=(), held_as=jnp.bfloat16):
    loudness = block_levels(rng, extent, cuts, -0.22, 0.18) if cuts else 1.0
    result = jax.random.normal(rng, extent, jnp.float32) * width * loudness
    return jnp.minimum(jnp.maximum(result, -bound), bound).astype(held_as)


def setup_inputs(seed: int = 0) -> dict:
    key_list = jax.random.split(jax.random.key(seed), 10)
    return {
        "head_input": normal_values(key_list[0], (TOKENS, INNER), 1.0, 6.0, ((0, 64), (1, 4))),
        "gate_input": draw_gate_input(jax.random.fold_in(key_list[9], 71), 0),
        "step_size": jnp.clip(jnp.exp(math.log(0.04) - 1.3862944 * jax.random.uniform(key_list[2], (TOKENS, H), jnp.float32) ** block_levels(key_list[2], (TOKENS, H), ((0, 64), (1, 4)), -0.2, 0.2)), 0.01, 0.04),
        "input_proj": normal_values(key_list[3], (TOKENS, N), 1.0, 6.0, ((0, 64),)),
        "output_proj": normal_values(key_list[4], (TOKENS, N), 1.0, 6.0, ((0, 64),)),
        "decay_rate": draw_decay_rate(jax.random.fold_in(key_list[9], 71), 0),
        "skip_gain": jnp.clip(0.5 + 1.0 * jax.random.uniform(key_list[6], (H,), jnp.float32) ** block_levels(key_list[6], (H,), ((0, 4),), -0.2, 0.2), 0.5, 1.5),
        "norm_gain": jnp.clip(1.0 + 0.1 * jax.random.normal(key_list[7], (INNER,), jnp.float32), 0.5, 1.5),
        "doc_lengths": uneven_parts(key_list[8], DOCS, TOKENS, TOKENS // 4, 2).astype(jnp.int32),
    }


def doc_number(positions, doc_ends):
    return lax.optimization_barrier(jnp.sum((doc_ends[None, :] <= positions[:, None]).astype(jnp.int32), axis=1)).astype(jnp.int32)

def decay_logs(block_step, decay_rate):
    return jnp.cumsum(-decay_rate[None, :] * block_step, axis=0)

def group_state(block_in, block_step, block_b, block_doc, before_doc, log_decay):
    final_log = log_decay[-1]
    tail_same = (block_doc == block_doc[-1])[:, None]
    weighting = jnp.where(tail_same, jnp.exp(final_log[None, :] - log_decay), 0.0) * block_step
    scaled_b = (weighting[:, :, None] * block_b.astype(jnp.float32)[:, None, :]).astype(jnp.bfloat16)
    scaled_b = lax.optimization_barrier(scaled_b)
    partial_state = jnp.einsum('qhp,qhn->hpn', block_in.astype(jnp.float32), scaled_b.astype(jnp.float32))
    passing = jnp.where(block_doc[-1] == before_doc, jnp.exp(final_log), 0.0)
    return (partial_state, passing)

def group_output(block_in, block_step, block_b, block_c, block_doc, before_doc, log_decay, entering, skip_gain):
    length = block_in.shape[0]
    scores = jnp.dot(block_c, block_b.T, preferred_element_type=jnp.float32)
    spread = log_decay.T[:, :, None] - log_decay.T[:, None, :]
    rows_idx = jnp.arange(length)[:, None]
    cols_idx = jnp.arange(length)[None, :]
    allowed = ((rows_idx >= cols_idx) & (block_doc[:, None] == block_doc[None, :]))[None]
    factor = jnp.where(allowed, jnp.exp(jnp.where(allowed, spread, 0.0)), 0.0)
    weights = (factor * scores[None] * block_step.T[:, None, :]).astype(jnp.bfloat16)
    weights = lax.optimization_barrier(weights)
    inside = jnp.einsum('hij,jhp->ihp', weights.astype(jnp.float32), block_in.astype(jnp.float32))
    states_bf16 = lax.optimization_barrier(entering.astype(jnp.bfloat16))
    entry_decay = jnp.where((block_doc == before_doc)[:, None], jnp.exp(log_decay), 0.0)
    carried = jnp.einsum('qn,hpn->qhp', block_c.astype(jnp.float32), states_bf16.astype(jnp.float32)) * entry_decay[:, :, None]
    return inside + carried + skip_gain[None, :, None] * block_in.astype(jnp.float32)

def reference(head_input, gate_input, step_size, input_proj, output_proj, decay_rate, skip_gain, norm_gain, doc_lengths):
    tokens_all = head_input.shape[0]
    head_count = step_size.shape[1]
    group_count = tokens_all // Q
    doc_ends = jnp.cumsum(doc_lengths).astype(jnp.int32)
    doc_ids = doc_number(jnp.arange(tokens_all, dtype=jnp.int32), doc_ends)
    befores = doc_number(jnp.arange(group_count, dtype=jnp.int32) * Q - 1, doc_ends)
    blocks_in = head_input.reshape(group_count, Q, head_count, P_SIZE)
    blocks_gate = gate_input.reshape(group_count, Q, head_count * P_SIZE)
    blocks_step = step_size.reshape(group_count, Q, head_count)
    blocks_b = input_proj.reshape(group_count, Q, N)
    blocks_c = output_proj.reshape(group_count, Q, N)
    blocks_doc = doc_ids.reshape(group_count, Q)

    def advance(carry_state, pieces):
        block_in, block_step, block_b, block_doc, before_doc = pieces
        log_decay = decay_logs(block_step, decay_rate)
        partial_state, passing = group_state(block_in, block_step, block_b, block_doc, before_doc, log_decay)
        return (passing[:, None, None] * carry_state + partial_state, carry_state)
    start_state = jnp.zeros((head_count, P_SIZE, N), jnp.float32)
    final_state, entering_all = lax.scan(advance, start_state, (blocks_in, blocks_step, blocks_b, blocks_doc, befores))

    def produce(pieces):
        block_in, block_gate, block_step, block_b, block_c, block_doc, before_doc, entering = pieces
        log_decay = decay_logs(block_step, decay_rate)
        mixed_rows = group_output(block_in, block_step, block_b, block_c, block_doc, before_doc, log_decay, entering, skip_gain)
        gated_rows = mixed_rows.reshape(Q, head_count * P_SIZE) * jax.nn.silu(block_gate.astype(jnp.float32))
        mean_square = lax.optimization_barrier(jnp.sum(gated_rows * gated_rows, axis=1)) / (head_count * P_SIZE)
        return (gated_rows * lax.rsqrt(mean_square + 1e-05)[:, None] * norm_gain[None, :]).astype(jnp.bfloat16)
    outputs = lax.map(produce, (blocks_in, blocks_gate, blocks_step, blocks_b, blocks_c, blocks_doc, befores, entering_all))
    return (outputs.reshape(tokens_all, head_count * P_SIZE), entering_all)
```

```python
import functools
import jax
import jax.numpy as jnp
from jax import lax
from jax.experimental import pallas as pl
from jax.experimental.pallas import tpu as pltpu
from jax.sharding import PartitionSpec as P

P_SIZE = 128
N = 128
Q = 256
F32 = jnp.float32
BF16 = jnp.bfloat16
Y_SIZE = 4
Z_SIZE = 8
NT = (((1,), (1,)), ((), ()))
TN = (((0,), (0,)), ((), ()))


def seq_index(y, z, core):
    return ((y % Y_SIZE) * Z_SIZE + (z % Z_SIZE)) * 2 + core


def seq_pairs(move):
    pairs = []
    for y in range(Y_SIZE):
        for z in range(Z_SIZE):
            for core in range(2):
                pairs.append((seq_index(y, z, core), seq_index(*move(y, z, core))))
    return pairs


CORE_SWAP = seq_pairs(lambda y, z, core: (y, z, 1 - core))
NEXT_ROW = seq_pairs(lambda y, z, core: (y + 1, z, core))
RINGS = [
    [seq_index(y, z, core) for z in range(Z_SIZE)] for y in range(Y_SIZE) for core in range(2)
]


def group_bounds(doc_ref, start):
    last = start + (Q - 1)
    doc_first = jnp.int32(0)
    next_end = jnp.int32(2147483647)
    end = jnp.int32(0)
    for k in range(doc_ref.shape[0]):
        end = end + doc_ref[k]
        doc_first = jnp.where(end <= last, end, doc_first)
        next_end = jnp.minimum(next_end, jnp.where(end >= start, end, 2147483647))
    return doc_first, next_end


def split3(values):
    high = values.astype(BF16)
    rest = values - high.astype(F32)
    mid = rest.astype(BF16)
    low = (rest - mid.astype(F32)).astype(BF16)
    return high, mid, low


def column_logs(step, rate_ref):
    head_rows = lax.broadcasted_iota(jnp.int32, step.shape, 0)
    terms = jnp.zeros_like(step)
    for head in range(step.shape[0]):
        terms = jnp.where(head_rows == head, -rate_ref[head] * step, terms)
    rows = lax.broadcasted_iota(jnp.int32, (Q, Q), 0)
    cols = lax.broadcasted_iota(jnp.int32, (Q, Q), 1)
    lower = jnp.where(cols <= rows, 1.0, 0.0).astype(BF16)
    return sum(
        lax.dot_general(lower, part, NT, preferred_element_type=F32) for part in split3(terms)
    )


def head_columns(values, head):
    return jnp.broadcast_to(values[:, head : head + 1], (values.shape[0], P_SIZE))


def scaled_pair(x, scale, pair):
    parts = []
    for head in (2 * pair, 2 * pair + 1):
        columns = x[:, head * P_SIZE : (head + 1) * P_SIZE].astype(F32)
        parts.append((columns * head_columns(scale, head)).astype(BF16))
    return jnp.concatenate(parts, axis=1)


def states_kernel(
    heads,
    groups,
    doc_hbm,
    rate_hbm,
    step_hbm,
    b_hbm,
    x_hbm,
    state_ref,
    before_ref,
    pass_ref,
    doc_ref,
    rate_ref,
    step_ref,
    b_ref,
    x_ref,
    small_sems,
    wide_sems,
):
    small = [
        pltpu.make_async_copy(src, dst, small_sems.at[i])
        for i, (src, dst) in enumerate(
            ((step_hbm, step_ref), (rate_hbm, rate_ref), (doc_hbm, doc_ref), (b_hbm, b_ref))
        )
    ]
    wide = [
        pltpu.make_async_copy(
            x_hbm.at[pl.ds(group * Q, Q), :], x_ref.at[group], wide_sems.at[group]
        )
        for group in range(groups)
    ]
    for copy in small + wide:
        copy.start()
    for copy in small:
        copy.wait()
    pass_ref[...] = jnp.ones_like(pass_ref)
    base = lax.axis_index("seq") * (groups * Q)
    prepared = []
    reach = jnp.ones((1, heads), F32)
    for group in range(groups):
        start = base + group * Q
        doc_first, next_end = group_bounds(doc_ref, start)
        step = step_ref[:, group * Q : (group + 1) * Q]
        logs = column_logs(step, rate_ref)
        scale = jnp.exp(-logs) * step.T
        final = jnp.exp(logs[Q - 1 : Q, :])
        passing = jnp.where(start + (Q - 1) < next_end, final, 0.0)
        positions = lax.broadcasted_iota(jnp.int32, (N, Q), 1) + start
        b_rows = b_ref[group * Q : (group + 1) * Q, :].astype(F32).T
        tail_b = jnp.where(positions >= doc_first, b_rows, 0.0).astype(BF16)
        reach = reach * passing
        pass_ref[group + 1 : group + 2, 0:heads] = reach
        prepared.append((scale, final, passing, tail_b))
    for head in range(heads):
        state_ref[head, N : N + 8, :] = jnp.broadcast_to(reach[:, head : head + 1], (8, P_SIZE))
    for group in range(groups):
        scale, final, passing, tail_b = prepared[group]
        wide[group].wait()
        x = x_ref.at[group]
        for pair in range(heads // 2):
            scaled = scaled_pair(x, scale, pair)
            product = jnp.dot(tail_b, scaled, preferred_element_type=F32)
            for part in range(2):
                head = 2 * pair + part
                state = product[:, part * P_SIZE : (part + 1) * P_SIZE] * final[:, head : head + 1]
                if group > 0:
                    state = state + before_ref[group - 1, head] * passing[:, head : head + 1]
                if group < groups - 1:
                    before_ref[group, head] = state
                else:
                    state_ref[head, 0:N, :] = state


def inside_kernel(
    heads,
    groups,
    doc_ref,
    rate_ref,
    skip_ref,
    step_ref,
    b_ref,
    c_ref,
    x_ref,
    gate_ref,
    after_ref,
    u_ref,
    v_ref,
):
    base = lax.axis_index("seq") * (groups * Q)
    rows = lax.broadcasted_iota(jnp.int32, (Q, Q), 0)
    cols = lax.broadcasted_iota(jnp.int32, (Q, Q), 1)
    for group in range(groups):
        start = base + group * Q
        block = slice(group * Q, (group + 1) * Q)
        _, next_end = group_bounds(doc_ref, start)
        step = step_ref[:, block]
        logs = column_logs(step, rate_ref)
        scale = jnp.exp(-logs) * step.T
        decay = jnp.exp(logs)
        positions = lax.broadcasted_iota(jnp.int32, (Q, heads), 0) + start
        entry = jnp.where(positions < next_end, decay, 0.0)
        first = jnp.zeros((Q, Q), jnp.int32)
        end = jnp.int32(0)
        for k in range(doc_ref.shape[0]):
            end = end + doc_ref[k]
            first = jnp.where(end - start <= rows, end - start, first)
        scores = lax.dot_general(c_ref[block, :], b_ref[block, :], NT, preferred_element_type=F32)
        masked = jnp.where((cols <= rows) & (cols >= first), scores, 0.0).astype(BF16)
        for pair in range(heads // 2):
            scaled = scaled_pair(x_ref.at[block, :], scale, pair)
            product = jnp.dot(masked, scaled, preferred_element_type=F32)
            for part in range(2):
                head = 2 * pair + part
                span = slice(head * P_SIZE, (head + 1) * P_SIZE)
                gate = gate_ref[block, span].astype(F32)
                active = gate / (1.0 + jnp.exp(-gate))
                inside = product[:, part * P_SIZE : (part + 1) * P_SIZE]
                inside = inside * head_columns(decay, head)
                inside = inside + skip_ref[head] * x_ref[block, span].astype(F32)
                u_ref[block, span] = inside * active
                v_ref[block, span] = head_columns(entry, head) * active


def join_cores_kernel(own_ref, other_ref, joined_ref):
    core = lax.rem(lax.axis_index("seq"), 2)
    half = joined_ref.shape[0]
    for slot in range(half):
        head = core * half + slot
        own, other = own_ref[head], other_ref[head]
        earlier = jnp.where(core == 0, own, other)
        later = jnp.where(core == 0, other, own)
        later_pass = later[N : N + 1, :]
        joined_ref[slot, 0:N, :] = later_pass * earlier[0:N, :] + later[0:N, :]
        joined_ref[slot, N : N + 8, :] = later_pass * earlier[N : N + 8, :]


def row_total_kernel(parts_ref, after_ref, total_ref):
    total = parts_ref[0, 0:N, :]
    for chip in range(1, Z_SIZE):
        total = parts_ref[chip, N : N + 1, :] * total + parts_ref[chip, 0:N, :]
    total_ref[...] = total


def entering_kernel(parts_ref, carried_ref, entering_ref):
    row = lax.axis_index("seq") // (2 * Z_SIZE)
    state = jnp.where(row > 0, carried_ref[...], 0.0)
    for chip in range(Z_SIZE):
        entering_ref[chip] = state
        if chip < Z_SIZE - 1:
            state = parts_ref[chip, N : N + 1, :] * state + parts_ref[chip, 0:N, :]


def outputs_kernel(
    heads,
    groups,
    own_ref,
    swapped_ref,
    other_ref,
    before_ref,
    pass_ref,
    c_ref,
    u_ref,
    v_ref,
    gated_ref,
    squares_ref,
    states_hbm,
    first_ref,
    states_ref,
    sems,
):
    core = lax.rem(lax.axis_index("seq"), 2)
    half = heads // 2
    for head in range(heads):
        here = core == (head // half)
        chip_state = jnp.where(here, own_ref[head % half], swapped_ref[head % half])
        joined = other_ref[head, N : N + 1, :] * chip_state + other_ref[head, 0:N, :]
        first_ref[head] = jnp.where(core == 0, chip_state, joined)
    ones = jnp.ones((8, P_SIZE), F32)
    copies = []
    for group in range(groups):
        block = slice(group * Q, (group + 1) * Q)
        reach = pass_ref[group : group + 1, 0:heads]
        squares = jnp.zeros((Q, P_SIZE), F32)
        for pair in range(heads // 2):
            both = []
            for part in range(2):
                head = 2 * pair + part
                state = first_ref[head]
                if group > 0:
                    state = state * reach[:, head : head + 1] + before_ref[group - 1, head]
                states_ref[group, head] = state.T
                both.append(state.astype(BF16))
            carried = jnp.dot(
                c_ref[block, :], jnp.concatenate(both, axis=1), preferred_element_type=F32
            )
            span = slice(2 * pair * P_SIZE, 2 * (pair + 1) * P_SIZE)
            gated = u_ref[block, span] + v_ref[block, span] * carried
            gated_ref[block, span] = gated
            square = gated * gated
            squares = squares + square[:, 0:P_SIZE] + square[:, P_SIZE:]
        copy = pltpu.make_async_copy(states_ref.at[group], states_hbm.at[group], sems.at[group])
        copy.start()
        copies.append(copy)
        squares_ref[:, block] = lax.dot_general(
            ones, squares, NT, precision=lax.Precision.HIGHEST, preferred_element_type=F32
        )
    for copy in copies:
        copy.wait()


SCALE_ROWS = 128


def scale_kernel(inner, gated_ref, gain_ref, own_ref, a_ref, b_ref, c_ref, out_hbm, out_ref, sems):
    mean = (own_ref[...] + a_ref[...] + b_ref[...] + c_ref[...]) * (1.0 / inner)
    scale = lax.rsqrt(mean + 1e-05)
    pick = jnp.where(lax.broadcasted_iota(jnp.int32, (8, P_SIZE), 0) == 0, 1.0, 0.0)
    copies = []
    for chunk in range(gated_ref.shape[0] // SCALE_ROWS):
        block = slice(chunk * SCALE_ROWS, (chunk + 1) * SCALE_ROWS)
        column = lax.dot_general(
            scale[:, block],
            pick,
            TN,
            precision=lax.Precision.HIGHEST,
            preferred_element_type=F32,
        )
        for tile in range(gated_ref.shape[1] // P_SIZE):
            span = slice(tile * P_SIZE, (tile + 1) * P_SIZE)
            out_ref[block, span] = (gated_ref[block, span] * column * gain_ref[:, span]).astype(
                BF16
            )
        copy = pltpu.make_async_copy(
            out_ref.at[pl.ds(chunk * SCALE_ROWS, SCALE_ROWS), :],
            out_hbm.at[pl.ds(chunk * SCALE_ROWS, SCALE_ROWS), :],
            sems.at[chunk],
        )
        copy.start()
        copies.append(copy)
    for copy in copies:
        copy.wait()


def cost(flops, bytes_accessed):
    return pl.CostEstimate(flops=flops, bytes_accessed=bytes_accessed, transcendentals=0)


def params(mebibytes):
    return pltpu.CompilerParams(vmem_limit_bytes=mebibytes * 1024 * 1024)


def local(
    head_input,
    gate_input,
    step_size,
    input_proj,
    output_proj,
    decay_rate,
    skip_gain,
    norm_gain,
    doc_lengths,
):
    row_count, width = head_input.shape
    heads = step_size.shape[1]
    half = heads // 2
    groups = row_count // Q
    sds = jax.ShapeDtypeStruct
    step_rows = step_size.T
    gain = norm_gain.reshape(1, width)
    smem = pl.BlockSpec(memory_space=pltpu.SMEM)
    vmem = pl.BlockSpec(memory_space=pltpu.VMEM)
    hbm = pl.BlockSpec(memory_space=pltpu.HBM)
    anywhere = pl.BlockSpec(memory_space=pl.ANY)
    dma = pltpu.SemaphoreType.DMA

    state, before, passes = pl.pallas_call(
        functools.partial(states_kernel, heads, groups),
        in_specs=[hbm] * 5,
        out_specs=[vmem] * 3,
        out_shape=[
            sds((heads, N + 8, P_SIZE), F32),
            sds((groups - 1, heads, N, P_SIZE), F32),
            sds((8, P_SIZE), F32),
        ],
        scratch_shapes=[
            pltpu.SMEM(doc_lengths.shape, jnp.int32),
            pltpu.SMEM(decay_rate.shape, F32),
            pltpu.VMEM((heads, row_count), F32),
            pltpu.VMEM((row_count, N), BF16),
            pltpu.VMEM((groups, Q, width), BF16),
            dma((4,)),
            dma((groups,)),
        ],
        compiler_params=params(24),
        cost_estimate=cost(400_000_000, 6_000_000),
        name="states",
    )(doc_lengths, decay_rate, step_rows, input_proj, head_input)

    other = lax.ppermute(state, "seq", CORE_SWAP)

    joined = pl.pallas_call(
        join_cores_kernel,
        out_shape=sds((half, N + 8, P_SIZE), F32),
        compiler_params=params(8),
        cost_estimate=cost(1_000_000, 1_700_000),
        name="join_cores",
    )(state, other)

    parts = lax.all_to_all(
        joined, "seq", split_axis=0, concat_axis=0, axis_index_groups=RINGS, tiled=True
    )

    u, v = pl.pallas_call(
        functools.partial(inside_kernel, heads, groups),
        in_specs=[smem, smem, smem, vmem, vmem, vmem, vmem, vmem, anywhere],
        out_specs=[vmem, vmem],
        out_shape=[sds((row_count, width), F32), sds((row_count, width), F32)],
        compiler_params=params(28),
        cost_estimate=cost(8_000_000_000, 20_000_000),
        name="inside",
    )(
        doc_lengths,
        decay_rate,
        skip_gain,
        step_rows,
        input_proj,
        output_proj,
        head_input,
        gate_input,
        joined,
    )

    total = pl.pallas_call(
        row_total_kernel,
        in_specs=[vmem, anywhere],
        out_shape=sds((N, P_SIZE), F32),
        compiler_params=params(8),
        cost_estimate=cost(300_000, 600_000),
        name="row_total",
    )(parts, u)
    carried = lax.ppermute(total, "seq", NEXT_ROW)
    entering = pl.pallas_call(
        entering_kernel,
        out_shape=sds((Z_SIZE, N, P_SIZE), F32),
        compiler_params=params(8),
        cost_estimate=cost(300_000, 1_100_000),
        name="entering",
    )(parts, carried)

    own = lax.all_to_all(
        entering, "seq", split_axis=0, concat_axis=0, axis_index_groups=RINGS, tiled=True
    )
    swapped = lax.ppermute(own, "seq", CORE_SWAP)

    gated, squares, group_states = pl.pallas_call(
        functools.partial(outputs_kernel, heads, groups),
        in_specs=[vmem] * 8,
        out_specs=[vmem, vmem, hbm],
        out_shape=[
            sds((row_count, width), F32),
            sds((8, row_count), F32),
            sds((groups, heads, P_SIZE, N), F32),
        ],
        scratch_shapes=[
            pltpu.VMEM((heads, N, P_SIZE), F32),
            pltpu.VMEM((groups, heads, P_SIZE, N), F32),
            dma((groups,)),
        ],
        compiler_params=params(34),
        cost_estimate=cost(400_000_000, 18_000_000),
        name="outputs",
    )(own, swapped, other, before, passes, output_proj, u, v)

    tp_size = 4
    sums = [
        lax.ppermute(squares, "tp", [(i, (i + k) % tp_size) for i in range(tp_size)])
        for k in range(1, tp_size)
    ]
    mixed_out = pl.pallas_call(
        functools.partial(scale_kernel, width * tp_size),
        in_specs=[vmem] * 6,
        out_specs=hbm,
        out_shape=sds((row_count, width), BF16),
        scratch_shapes=[pltpu.VMEM((row_count, width), BF16), dma((row_count // SCALE_ROWS,))],
        compiler_params=params(16),
        cost_estimate=cost(5_000_000, 6_500_000),
        name="scale",
    )(gated, gain, squares, *sums)
    return (mixed_out, group_states)


def solution(mesh):
    return jax.shard_map(
        local,
        mesh=mesh,
        in_specs=(
            P("seq", "tp"),
            P("seq", "tp"),
            P("seq", "tp"),
            P("seq", None),
            P("seq", None),
            P("tp"),
            P("tp"),
            P("tp"),
            P(),
        ),
        out_specs=(P("seq", "tp"), P("seq", "tp", None, None)),
        check_vma=False,
    )
```

```python
import functools
import jax
import jax.numpy as jnp
from jax import lax
from jax.experimental import pallas as pl
from jax.experimental.pallas import tpu as pltpu
from jax.sharding import PartitionSpec as P

P_SIZE = 128
N = 128
Q = 256
F32 = jnp.float32
BF16 = jnp.bfloat16
Y_SIZE = 4
Z_SIZE = 8
NT = (((1,), (1,)), ((), ()))


def seq_index(y, z, core):
    return ((y % Y_SIZE) * Z_SIZE + (z % Z_SIZE)) * 2 + core


def seq_pairs(move):
    pairs = []
    for y in range(Y_SIZE):
        for z in range(Z_SIZE):
            for core in range(2):
                pairs.append((seq_index(y, z, core), seq_index(*move(y, z, core))))
    return pairs


CORE_SWAP = seq_pairs(lambda y, z, core: (y, z, 1 - core))
NEXT_ROW = seq_pairs(lambda y, z, core: (y + 1, z, core))
RINGS = [
    [seq_index(y, z, core) for z in range(Z_SIZE)] for y in range(Y_SIZE) for core in range(2)
]


def group_bounds(doc_ref, start):
    last = start + (Q - 1)
    doc_first = jnp.int32(0)
    next_end = jnp.int32(2147483647)
    end = jnp.int32(0)
    for k in range(doc_ref.shape[0]):
        end = end + doc_ref[k]
        doc_first = jnp.where(end <= last, end, doc_first)
        next_end = jnp.minimum(next_end, jnp.where(end >= start, end, 2147483647))
    return doc_first, next_end


def split3(values):
    high = values.astype(BF16)
    rest = values - high.astype(F32)
    mid = rest.astype(BF16)
    low = (rest - mid.astype(F32)).astype(BF16)
    return high, mid, low


def core_index():
    return lax.rem(lax.axis_index("seq"), 2)


def head_of(slot, heads):
    return lax.rem(slot + core_index() * (heads // 2), heads)


def head_span(slot, heads, count=1):
    return pl.ds(pl.multiple_of(head_of(slot, heads) * P_SIZE, P_SIZE), count * P_SIZE)


def slot_rows(rows):
    half = rows.shape[0] // 2
    turned = jnp.concatenate([rows[half:], rows[:half]], axis=0)
    return jnp.where(core_index() == 0, rows, turned)


def column_logs(step, rate_ref):
    head_rows = lax.broadcasted_iota(jnp.int32, step.shape, 0)
    terms = jnp.zeros_like(step)
    for head in range(step.shape[0]):
        terms = jnp.where(head_rows == head, -rate_ref[head_of(head, step.shape[0])] * step, terms)
    rows = lax.broadcasted_iota(jnp.int32, (Q, Q), 0)
    cols = lax.broadcasted_iota(jnp.int32, (Q, Q), 1)
    lower = jnp.where(cols <= rows, 1.0, 0.0).astype(BF16)
    return sum(
        lax.dot_general(lower, part, NT, preferred_element_type=F32) for part in split3(terms)
    )


def head_columns(values, head):
    return jnp.broadcast_to(values[:, head : head + 1], (values.shape[0], P_SIZE))


def scaled_pair(x, scale, slot, heads):
    parts = []
    for part in range(2):
        columns = x[:, part * P_SIZE : (part + 1) * P_SIZE].astype(F32)
        parts.append((columns * head_columns(scale, slot + part)).astype(BF16))
    return jnp.concatenate(parts, axis=1)


def half_states(groups, first_slot, x_of, scale_of, tail_of, stats_ref, state_ref):
    half = state_ref.shape[0]
    for group in range(groups):
        final = stats_ref[group : group + 1, :]
        passing = stats_ref[8 + group : 9 + group, :]
        tail_b = tail_of(group)
        scale = scale_of(group)
        for pair in range(half // 2):
            slot = first_slot + 2 * pair
            scaled = scaled_pair(x_of(group, pair), scale, slot, 2 * half)
            product = jnp.dot(tail_b, scaled, preferred_element_type=F32)
            for part in range(2):
                lane = slice(slot + part, slot + part + 1)
                index = 2 * pair + part
                state = product[:, part * P_SIZE : (part + 1) * P_SIZE] * final[:, lane]
                if group > 0:
                    state = state + state_ref[index, 0:N, :] * passing[:, lane]
                state_ref[index, 0:N, :] = state
    reach = stats_ref[16 + groups : 17 + groups, :]
    for index in range(half):
        lane = slice(first_slot + index, first_slot + index + 1)
        state_ref[index, N : N + 8, :] = jnp.broadcast_to(reach[:, lane], (8, P_SIZE))


def away_states_kernel(
    heads,
    groups,
    doc_hbm,
    rate_hbm,
    step_hbm,
    b_hbm,
    x_hbm,
    state_ref,
    stats_ref,
    scale_ref,
    tail_ref,
    doc_ref,
    rate_ref,
    step_ref,
    b_ref,
    x_ref,
    small_sems,
    wide_sems,
):
    half = heads // 2
    small = [
        pltpu.make_async_copy(src, dst, small_sems.at[i])
        for i, (src, dst) in enumerate(
            ((step_hbm, step_ref), (rate_hbm, rate_ref), (doc_hbm, doc_ref), (b_hbm, b_ref))
        )
    ]
    wide = [
        pltpu.make_async_copy(
            x_hbm.at[pl.ds(group * Q, Q), head_span(half, heads, half)],
            x_ref.at[group],
            wide_sems.at[group],
        )
        for group in range(groups)
    ]
    for copy in small + wide:
        copy.start()
    for copy in small:
        copy.wait()
    stats_ref[...] = jnp.zeros_like(stats_ref)
    base = lax.axis_index("seq") * (groups * Q)
    reach = jnp.ones((1, heads), F32)
    stats_ref[16:17, 0:heads] = reach
    for group in range(groups):
        start = base + group * Q
        doc_first, next_end = group_bounds(doc_ref, start)
        step = slot_rows(step_ref[:, group * Q : (group + 1) * Q])
        logs = column_logs(step, rate_ref)
        scale_ref[group] = jnp.exp(-logs) * step.T
        final = jnp.exp(logs[Q - 1 : Q, :])
        passing = jnp.where(start + (Q - 1) < next_end, final, 0.0)
        positions = lax.broadcasted_iota(jnp.int32, (N, Q), 1) + start
        b_rows = b_ref[group * Q : (group + 1) * Q, :].astype(F32).T
        tail_ref[group] = jnp.where(positions >= doc_first, b_rows, 0.0).astype(BF16)
        reach = reach * passing
        stats_ref[group : group + 1, 0:heads] = final
        stats_ref[8 + group : 9 + group, 0:heads] = passing
        stats_ref[17 + group : 18 + group, 0:heads] = reach

    def x_of(group, pair):
        if pair == 0:
            wide[group].wait()
        return x_ref[group, :, 2 * pair * P_SIZE : 2 * (pair + 1) * P_SIZE]

    half_states(
        groups,
        half,
        x_of,
        lambda group: scale_ref[group],
        lambda group: tail_ref[group],
        stats_ref,
        state_ref,
    )


def own_states_kernel(heads, groups, stats_ref, scale_ref, tail_ref, x_ref, state_ref):
    half_states(
        groups,
        0,
        lambda group, pair: x_ref[group * Q : (group + 1) * Q, head_span(2 * pair, heads, 2)],
        lambda group: scale_ref[group],
        lambda group: tail_ref[group],
        stats_ref,
        state_ref,
    )


def inside_kernel(
    heads,
    groups,
    doc_hbm,
    rate_hbm,
    skip_hbm,
    step_hbm,
    b_hbm,
    c_hbm,
    x_hbm,
    gate_hbm,
    after_ref,
    own_u_hbm,
    own_v_hbm,
    away_u_hbm,
    away_v_hbm,
    own_before_hbm,
    away_before_hbm,
    entry_c_hbm,
    token_ref,
    own_u_ref,
    own_v_ref,
    away_u_ref,
    away_v_ref,
    own_before_ref,
    away_before_ref,
    entry_c_ref,
    out_sems,
    doc_ref,
    rate_ref,
    skip_ref,
    step_ref,
    b_ref,
    c_ref,
    x_ref,
    gate_ref,
    small_sems,
    wide_sems,
):
    small = [
        pltpu.make_async_copy(src, dst, small_sems.at[i])
        for i, (src, dst) in enumerate(
            (
                (step_hbm, step_ref),
                (rate_hbm, rate_ref),
                (doc_hbm, doc_ref),
                (skip_hbm, skip_ref),
                (b_hbm, b_ref),
                (c_hbm, c_ref),
            )
        )
    ]
    wide = []
    for group in range(groups):
        for side, (src, dst) in enumerate(((x_hbm, x_ref), (gate_hbm, gate_ref))):
            wide.append(
                pltpu.make_async_copy(
                    src.at[pl.ds(group * Q, Q), :],
                    dst.at[pl.ds(group * Q, Q), :],
                    wide_sems.at[group, side],
                )
            )
    for copy in small + wide:
        copy.start()
    for copy in small:
        copy.wait()
    half = heads // 2
    copies, results = [], []
    base = lax.axis_index("seq") * (groups * Q)
    rows = lax.broadcasted_iota(jnp.int32, (Q, Q), 0)
    cols = lax.broadcasted_iota(jnp.int32, (Q, Q), 1)
    for group in range(groups):
        start = base + group * Q
        block = slice(group * Q, (group + 1) * Q)
        doc_first, next_end = group_bounds(doc_ref, start)
        step = slot_rows(step_ref[:, block])
        logs = column_logs(step, rate_ref)
        scale = jnp.exp(-logs) * step.T
        decay = jnp.exp(logs)
        final = decay[Q - 1 : Q, :]
        passing = jnp.where(start + (Q - 1) < next_end, final, 0.0)
        positions = lax.broadcasted_iota(jnp.int32, (Q, N), 0) + start
        entry_c = jnp.where(positions < next_end, c_ref[block, :].astype(F32), 0.0)
        entry_c_ref[block, :] = entry_c.astype(BF16)
        first = jnp.zeros((Q, Q), jnp.int32)
        end = jnp.int32(0)
        for k in range(doc_ref.shape[0]):
            end = end + doc_ref[k]
            first = jnp.where(end - start <= rows, end - start, first)
        scores = lax.dot_general(c_ref[block, :], b_ref[block, :], NT, preferred_element_type=F32)
        masked = jnp.where((cols <= rows) & (cols >= first), scores, 0.0).astype(BF16)
        lanes = lax.broadcasted_iota(jnp.int32, (N, Q), 1) + start
        tail_b = jnp.where(lanes >= doc_first, b_ref[block, :].astype(F32).T, 0.0).astype(BF16)
        wide[2 * group].wait()
        wide[2 * group + 1].wait()
        for pair in range(half):
            x = x_ref[block, head_span(2 * pair, heads, 2)]
            gates = gate_ref[block, head_span(2 * pair, heads, 2)]
            scaled = scaled_pair(x, scale, 2 * pair, heads)
            product = jnp.dot(masked, scaled, preferred_element_type=F32)
            if pair < half // 2:
                u_ref, v_ref, before_ref = own_u_ref, own_v_ref, own_before_ref
            else:
                u_ref, v_ref, before_ref = away_u_ref, away_v_ref, away_before_ref
            if group < groups - 1:
                states = jnp.dot(tail_b, scaled, preferred_element_type=F32)
            for part in range(2):
                slot = 2 * pair + part
                here = slice(part * P_SIZE, (part + 1) * P_SIZE)
                place = slot % half
                span = slice(place * P_SIZE, (place + 1) * P_SIZE)
                gate = 0.5 * gates[:, here].astype(F32)
                active = gate + gate * jnp.tanh(gate)
                carry = head_columns(decay, slot) * active
                direct = skip_ref[head_of(slot, heads)] * x[:, here].astype(F32)
                u_ref[block, span] = product[:, here] * carry + direct * active
                v_ref[block, span] = carry
                if group < groups - 1:
                    state = states[:, here] * final[:, slot : slot + 1]
                    if group > 0:
                        earlier = before_ref[group - 1, place]
                        state = state + earlier * passing[:, slot : slot + 1]
                    before_ref[group, place] = state
            if pair == half // 2 - 1:
                results.append((own_u_ref, own_u_hbm, 0))
                results.append((own_v_ref, own_v_hbm, 1))
                results.append((own_before_ref, own_before_hbm, 2))
            if pair == half - 1:
                results.append((away_u_ref, away_u_hbm, 3))
                results.append((away_v_ref, away_v_hbm, 4))
                results.append((away_before_ref, away_before_hbm, 5))
                results.append((entry_c_ref, entry_c_hbm, 6))
            for src, dst, index in results:
                if len(dst.shape) == 2:
                    where = pl.ds(group * Q, Q)
                elif group < groups - 1:
                    where = group
                else:
                    continue
                copy = pltpu.make_async_copy(
                    src.at[where], dst.at[where], out_sems.at[group, index]
                )
                copy.start()
                copies.append(copy)
            results = []
    for copy in copies:
        copy.wait()
    token_ref[...] = jnp.zeros_like(token_ref)


def join_cores_kernel(own_ref, other_ref, joined_ref, token_ref):
    core = core_index()
    for slot in range(joined_ref.shape[0]):
        own, other = own_ref[slot], other_ref[slot]
        earlier = jnp.where(core == 0, own, other)
        later = jnp.where(core == 0, other, own)
        later_pass = later[N : N + 1, :]
        joined_ref[slot, 0:N, :] = later_pass * earlier[0:N, :] + later[0:N, :]
        joined_ref[slot, N : N + 8, :] = later_pass * earlier[N : N + 8, :]
    token_ref[...] = jnp.zeros_like(token_ref)


def row_total_kernel(parts_ref, inside_ref, swap_ref, total_ref):
    total = parts_ref[0, 0:N, :]
    for chip in range(1, Z_SIZE):
        total = parts_ref[chip, N : N + 1, :] * total + parts_ref[chip, 0:N, :]
    total_ref[...] = total


def entering_kernel(parts_ref, carried_ref, entering_ref):
    row = lax.axis_index("seq") // (2 * Z_SIZE)
    state = jnp.where(row > 0, carried_ref[...], 0.0)
    for chip in range(Z_SIZE):
        entering_ref[chip] = state
        if chip < Z_SIZE - 1:
            state = parts_ref[chip, N : N + 1, :] * state + parts_ref[chip, 0:N, :]


def half_outputs_kernel(
    groups,
    first_slot,
    last,
    chip_ref,
    other_ref,
    before_ref,
    stats_ref,
    c_ref,
    u_ref,
    v_ref,
    sums_ref,
    gated_ref,
    squares_ref,
    first_ref,
):
    core = core_index()
    half = chip_ref.shape[0]
    for index in range(half):
        chip_state = chip_ref[index]
        joined = other_ref[index, N : N + 1, :] * chip_state + other_ref[index, 0:N, :]
        first_ref[index] = jnp.where(core == 0, chip_state, joined)
    for group in range(groups):
        block = slice(group * Q, (group + 1) * Q)
        reach = stats_ref[16 + group : 17 + group, :]
        squares = sums_ref[block, :] if last else jnp.zeros((Q, P_SIZE), F32)
        for pair in range(half // 2):
            both = []
            for index in (2 * pair, 2 * pair + 1):
                state = first_ref[index]
                if group > 0:
                    lane = slice(first_slot + index, first_slot + index + 1)
                    state = state * reach[:, lane] + before_ref[group - 1, index]
                both.append(state.astype(BF16))
            carried = jnp.dot(
                c_ref[block, :], jnp.concatenate(both, axis=1), preferred_element_type=F32
            )
            span = slice(2 * pair * P_SIZE, 2 * (pair + 1) * P_SIZE)
            gated = u_ref[block, span] + v_ref[block, span] * carried
            gated_ref[block, span] = gated
            square = gated * gated
            squares = squares + square[:, 0:P_SIZE] + square[:, P_SIZE:]
        if last:
            squares_ref[:, block] = jnp.broadcast_to(
                jnp.sum(squares.T, axis=0, keepdims=True), (8, Q)
            )
        else:
            squares_ref[block, :] = squares


def write_states_kernel(
    heads,
    groups,
    own_first_ref,
    away_first_ref,
    own_before_ref,
    away_before_ref,
    stats_ref,
    after_ref,
    states_hbm,
    token_ref,
    states_ref,
    sems,
):
    half = heads // 2
    copies = []
    for group in range(groups):
        reach = stats_ref[16 + group : 17 + group, :]
        for side, (first_ref, before_ref) in enumerate(
            ((own_first_ref, own_before_ref), (away_first_ref, away_before_ref))
        ):
            for index in range(half):
                state = first_ref[index]
                if group > 0:
                    slot = side * half + index
                    state = state * reach[:, slot : slot + 1] + before_ref[group - 1, index]
                states_ref[group, side, index] = state.T
            copy = pltpu.make_async_copy(
                states_ref.at[group, side],
                states_hbm.at[group, pl.ds(head_of(side * half, heads), half)],
                sems.at[group, side],
            )
            copy.start()
            copies.append(copy)
    for copy in copies:
        copy.wait()
    token_ref[...] = jnp.zeros_like(token_ref)


SCALE_ROWS = 128


def scale_kernel(
    inner, heads, own_ref, away_ref, gain_ref, sum_ref, a_ref, b_ref, c_ref, after_ref, out_hbm, out_ref, sems
):
    mean = (sum_ref[...] + a_ref[...] + b_ref[...] + c_ref[...]) * (1.0 / inner)
    scale = lax.rsqrt(mean + 1e-05)
    half = heads // 2
    copies = []
    for chunk in range(own_ref.shape[0] // SCALE_ROWS):
        block = slice(chunk * SCALE_ROWS, (chunk + 1) * SCALE_ROWS)
        column = jnp.broadcast_to(scale[0:1, block], (P_SIZE, SCALE_ROWS)).T
        for side, gated_ref in enumerate((own_ref, away_ref)):
            for index in range(half):
                span = slice(index * P_SIZE, (index + 1) * P_SIZE)
                gain = gain_ref[:, head_span(side * half + index, heads)]
                out_ref[side, block, span] = (gated_ref[block, span] * column * gain).astype(BF16)
            copy = pltpu.make_async_copy(
                out_ref.at[side, pl.ds(chunk * SCALE_ROWS, SCALE_ROWS), :],
                out_hbm.at[
                    pl.ds(chunk * SCALE_ROWS, SCALE_ROWS), head_span(side * half, heads, half)
                ],
                sems.at[side, chunk],
            )
            copy.start()
            copies.append(copy)
    for copy in copies:
        copy.wait()


def cost(flops, bytes_accessed):
    return pl.CostEstimate(flops=flops, bytes_accessed=bytes_accessed, transcendentals=0)


def params(mebibytes):
    return pltpu.CompilerParams(vmem_limit_bytes=mebibytes * 1024 * 1024)


def local(
    head_input,
    gate_input,
    step_size,
    input_proj,
    output_proj,
    decay_rate,
    skip_gain,
    norm_gain,
    doc_lengths,
):
    row_count, width = head_input.shape
    heads = step_size.shape[1]
    half = heads // 2
    groups = row_count // Q
    sds = jax.ShapeDtypeStruct
    step_rows = step_size.T
    gain = norm_gain.reshape(1, width)
    smem = pl.BlockSpec(memory_space=pltpu.SMEM)
    vmem = pl.BlockSpec(memory_space=pltpu.VMEM)
    hbm = pl.BlockSpec(memory_space=pltpu.HBM)
    anywhere = pl.BlockSpec(memory_space=pl.ANY)
    dma = pltpu.SemaphoreType.DMA

    token = sds((8, P_SIZE), F32)
    half_state = sds((half, N + 8, P_SIZE), F32)
    half_before = sds((groups - 1, half, N, P_SIZE), F32)
    half_wide = sds((row_count, width // 2), F32)
    half_first = sds((half, N, P_SIZE), F32)

    def in_hbm(*arrays):
        return [pltpu.with_memory_space_constraint(array, pltpu.HBM) for array in arrays]

    away_state, stats, scale, tail = pl.pallas_call(
        functools.partial(away_states_kernel, heads, groups),
        in_specs=[hbm] * 5,
        out_specs=[vmem] * 4,
        out_shape=[
            half_state,
            sds((24, P_SIZE), F32),
            sds((groups, Q, heads), F32),
            sds((groups, N, Q), BF16),
        ],
        scratch_shapes=[
            pltpu.SMEM(doc_lengths.shape, jnp.int32),
            pltpu.SMEM(decay_rate.shape, F32),
            pltpu.VMEM((heads, row_count), F32),
            pltpu.VMEM((row_count, N), BF16),
            pltpu.VMEM((groups, Q, width // 2), BF16),
            dma((4,)),
            dma((groups,)),
        ],
        compiler_params=params(16),
        cost_estimate=cost(200_000_000, 4_000_000),
        name="away_states",
    )(*in_hbm(doc_lengths, decay_rate, step_rows, input_proj, head_input))
    own_other = lax.ppermute(away_state, "seq", CORE_SWAP)

    own_state = pl.pallas_call(
        functools.partial(own_states_kernel, heads, groups),
        in_specs=[vmem] * 4,
        out_specs=vmem,
        out_shape=half_state,
        compiler_params=params(16),
        cost_estimate=cost(2_000_000_000, 4_000_000),
        name="own_states",
    )(stats, scale, tail, head_input)

    joined, joined_token = pl.pallas_call(
        join_cores_kernel,
        out_shape=[half_state, token],
        compiler_params=params(8),
        cost_estimate=cost(1_000_000, 1_700_000),
        name="join_cores",
    )(own_state, own_other)
    parts = lax.all_to_all(
        joined, "seq", split_axis=0, concat_axis=0, axis_index_groups=RINGS, tiled=True
    )
    away_other = lax.ppermute(own_state, "seq", CORE_SWAP)

    own_u, own_v, away_u, away_v, own_before, away_before, entry_c, inside_token = pl.pallas_call(
        functools.partial(inside_kernel, heads, groups),
        in_specs=[hbm] * 8 + [anywhere],
        out_specs=[hbm] * 7 + [vmem],
        out_shape=[pltpu.HBM(half_wide.shape, F32)] * 4
        + [pltpu.HBM(half_before.shape, F32)] * 2
        + [pltpu.HBM((row_count, N), BF16), token],
        scratch_shapes=[pltpu.VMEM(half_wide.shape, F32)] * 4
        + [pltpu.VMEM(half_before.shape, F32)] * 2
        + [pltpu.VMEM((row_count, N), BF16), dma((groups, 7))]
        + [
            pltpu.SMEM(doc_lengths.shape, jnp.int32),
            pltpu.SMEM(decay_rate.shape, F32),
            pltpu.SMEM(skip_gain.shape, F32),
            pltpu.VMEM((heads, row_count), F32),
            pltpu.VMEM((row_count, N), BF16),
            pltpu.VMEM((row_count, N), BF16),
            pltpu.VMEM((row_count, width), BF16),
            pltpu.VMEM((row_count, width), BF16),
            dma((6,)),
            dma((groups, 2)),
        ],
        compiler_params=params(36),
        cost_estimate=cost(8_000_000_000, 20_000_000),
        name="inside",
    )(
        *in_hbm(
            doc_lengths,
            decay_rate,
            skip_gain,
            step_rows,
            input_proj,
            output_proj,
            head_input,
            gate_input,
        ),
        joined_token,
    )
    total = pl.pallas_call(
        row_total_kernel,
        in_specs=[vmem, anywhere, anywhere],
        out_shape=sds((N, P_SIZE), F32),
        compiler_params=params(8),
        cost_estimate=cost(300_000, 600_000),
        name="row_total",
    )(parts, inside_token, away_other)
    carried = lax.ppermute(total, "seq", NEXT_ROW)
    entering = pl.pallas_call(
        entering_kernel,
        out_shape=sds((Z_SIZE, N, P_SIZE), F32),
        compiler_params=params(8),
        cost_estimate=cost(20_000_000_000, 1_100_000),
        name="entering",
    )(parts, carried)

    own_chip = lax.all_to_all(
        entering, "seq", split_axis=0, concat_axis=0, axis_index_groups=RINGS, tiled=True
    )

    away_chip = lax.ppermute(own_chip, "seq", CORE_SWAP)

    def half_outputs(first_slot, last, *operands):
        sums = sds((8, row_count), F32) if last else sds((row_count, P_SIZE), F32)
        return pl.pallas_call(
            functools.partial(half_outputs_kernel, groups, first_slot, last),
            in_specs=[vmem] * 7 + [vmem if last else anywhere],
            out_specs=[vmem] * 3,
            out_shape=[half_wide, sums, half_first],
            compiler_params=params(20),
            cost_estimate=cost(2_000_000_000, 9_000_000),
            name="away_outputs" if last else "own_outputs",
        )(*operands)

    own_gated, own_squares, own_first = half_outputs(
        0, False, own_chip, own_other, own_before, stats, entry_c, own_u, own_v, stats
    )
    away_gated, squares, away_first = half_outputs(
        half,
        True,
        away_chip,
        away_other,
        away_before,
        stats,
        entry_c,
        away_u,
        away_v,
        own_squares,
    )

    tp_size = 4
    sums = [
        lax.ppermute(squares, "tp", [(i, (i + k) % tp_size) for i in range(tp_size)])
        for k in range(1, tp_size)
    ]
    group_states, states_token = pl.pallas_call(
        functools.partial(write_states_kernel, heads, groups),
        in_specs=[vmem] * 5 + [anywhere],
        out_specs=[hbm, vmem],
        out_shape=[sds((groups, heads, P_SIZE, N), F32), token],
        scratch_shapes=[
            pltpu.VMEM((groups, 2, half, P_SIZE, N), F32),
            dma((groups, 2)),
        ],
        compiler_params=params(16),
        cost_estimate=cost(4_000_000_000, 9_000_000),
        name="write_states",
    )(own_first, away_first, own_before, away_before, stats, squares)
    mixed_out = pl.pallas_call(
        functools.partial(scale_kernel, width * tp_size, heads),
        in_specs=[vmem] * 7 + [anywhere],
        out_specs=hbm,
        out_shape=sds((row_count, width), BF16),
        scratch_shapes=[
            pltpu.VMEM((2, row_count, width // 2), BF16),
            dma((2, row_count // SCALE_ROWS)),
        ],
        compiler_params=params(16),
        cost_estimate=cost(5_000_000, 6_500_000),
        name="scale",
    )(own_gated, away_gated, gain, squares, *sums, states_token)
    return (mixed_out, group_states)


def solution(mesh):
    return jax.shard_map(
        local,
        mesh=mesh,
        in_specs=(
            P("seq", "tp"),
            P("seq", "tp"),
            P("seq", "tp"),
            P("seq", None),
            P("seq", None),
            P("tp"),
            P("tp"),
            P("tp"),
            P(),
        ),
        out_specs=(P("seq", "tp"), P("seq", "tp", None, None)),
        check_vma=False,
    )
```

```python
import functools
import jax
import jax.numpy as jnp
from jax import lax
from jax.experimental import pallas as pl
from jax.experimental.pallas import tpu as pltpu
from jax.sharding import PartitionSpec as P

P_SIZE = 128
N = 128
Q = 256
F32 = jnp.float32
BF16 = jnp.bfloat16
Y_SIZE = 4
Z_SIZE = 8
NT = (((1,), (1,)), ((), ()))


def seq_index(y, z, core):
    return ((y % Y_SIZE) * Z_SIZE + (z % Z_SIZE)) * 2 + core


def seq_pairs(move):
    pairs = []
    for y in range(Y_SIZE):
        for z in range(Z_SIZE):
            for core in range(2):
                pairs.append((seq_index(y, z, core), seq_index(*move(y, z, core))))
    return pairs


CORE_SWAP = seq_pairs(lambda y, z, core: (y, z, 1 - core))
NEXT_ROW = seq_pairs(lambda y, z, core: (y + 1, z, core))
NEXT_ROW_SWAP = seq_pairs(lambda y, z, core: (y + 1, z, 1 - core))
AROUND = [
    seq_pairs(lambda y, z, core, step=step: (y, z + (step if core == 0 else -step), core))
    for step in range(1, 5)
]
RINGS = [
    [seq_index(y, z, core) for z in range(Z_SIZE)] for y in range(Y_SIZE) for core in range(2)
]


def group_bounds(doc_ref, start):
    last = start + (Q - 1)
    doc_first = jnp.int32(0)
    next_end = jnp.int32(2147483647)
    end = jnp.int32(0)
    for k in range(doc_ref.shape[0]):
        end = end + doc_ref[k]
        doc_first = jnp.where(end <= last, end, doc_first)
        next_end = jnp.minimum(next_end, jnp.where(end >= start, end, 2147483647))
    return doc_first, next_end


def split3(values):
    high = values.astype(BF16)
    rest = values - high.astype(F32)
    mid = rest.astype(BF16)
    low = (rest - mid.astype(F32)).astype(BF16)
    return high, mid, low


def core_index():
    return lax.rem(lax.axis_index("seq"), 2)


def head_of(slot, heads):
    return lax.rem(slot + core_index() * (heads // 2), heads)


def head_span(slot, heads, count=1):
    return pl.ds(pl.multiple_of(head_of(slot, heads) * P_SIZE, P_SIZE), count * P_SIZE)


def slot_rows(rows):
    half = rows.shape[0] // 2
    turned = jnp.concatenate([rows[half:], rows[:half]], axis=0)
    return jnp.where(core_index() == 0, rows, turned)


def stacked_groups(rows):
    groups = rows.shape[1] // Q
    return jnp.concatenate([rows[:, g * Q : (g + 1) * Q] for g in range(groups)], axis=0)


def column_logs(step, rate_ref, heads):
    head_rows = lax.rem(lax.broadcasted_iota(jnp.int32, step.shape, 0), heads)
    rates = jnp.zeros_like(step)
    for slot in range(heads):
        rates = jnp.where(head_rows == slot, -rate_ref[head_of(slot, heads)], rates)
    rows = lax.broadcasted_iota(jnp.int32, (Q, Q), 0)
    cols = lax.broadcasted_iota(jnp.int32, (Q, Q), 1)
    lower = jnp.where(cols <= rows, 1.0, 0.0).astype(BF16)
    return sum(
        lax.dot_general(lower, part, NT, preferred_element_type=F32)
        for part in split3(rates * step)
    )


def head_columns(values, head):
    return jnp.broadcast_to(values[:, head : head + 1], (values.shape[0], P_SIZE))


def scaled_pair(x, scale, slot, heads):
    parts = []
    for part in range(2):
        columns = x[:, part * P_SIZE : (part + 1) * P_SIZE].astype(F32)
        parts.append((columns * head_columns(scale, slot + part)).astype(BF16))
    return jnp.concatenate(parts, axis=1)


def half_states(groups, first_slot, x_of, scale_ref, tail_of, stats_ref, state_ref):
    half = state_ref.shape[0]
    for group in range(groups):
        final = stats_ref[group : group + 1, :]
        passing = stats_ref[8 + group : 9 + group, :]
        tail_b = tail_of(group)
        scale = scale_ref[:, group * 2 * half : (group + 1) * 2 * half]
        for pair in range(half // 2):
            slot = first_slot + 2 * pair
            scaled = scaled_pair(x_of(group, pair), scale, slot, 2 * half)
            product = jnp.dot(tail_b, scaled, preferred_element_type=F32)
            for part in range(2):
                lane = slice(slot + part, slot + part + 1)
                index = 2 * pair + part
                state = product[:, part * P_SIZE : (part + 1) * P_SIZE] * final[:, lane]
                if group > 0:
                    state = state + state_ref[index, 0:N, :] * passing[:, lane]
                state_ref[index, 0:N, :] = state
    reach = stats_ref[16 + groups : 17 + groups, :]
    for index in range(half):
        lane = slice(first_slot + index, first_slot + index + 1)
        state_ref[index, N : N + 8, :] = jnp.broadcast_to(reach[:, lane], (8, P_SIZE))


def away_states_kernel(
    heads,
    groups,
    doc_hbm,
    rate_hbm,
    step_hbm,
    b_hbm,
    x_hbm,
    state_ref,
    stats_ref,
    scale_ref,
    tail_ref,
    doc_ref,
    rate_ref,
    step_ref,
    b_ref,
    x_ref,
    small_sems,
    wide_sems,
):
    half = heads // 2
    small = [
        pltpu.make_async_copy(src, dst, small_sems.at[i])
        for i, (src, dst) in enumerate(
            ((step_hbm, step_ref), (rate_hbm, rate_ref), (doc_hbm, doc_ref), (b_hbm, b_ref))
        )
    ]
    wide = [
        pltpu.make_async_copy(
            x_hbm.at[pl.ds(group * Q, Q), head_span(half, heads, half)],
            x_ref.at[group],
            wide_sems.at[group],
        )
        for group in range(groups)
    ]
    for copy in small + wide:
        copy.start()
    for copy in small:
        copy.wait()
    stats_ref[...] = jnp.zeros_like(stats_ref)
    base = lax.axis_index("seq") * (groups * Q)
    reach = jnp.ones((1, heads), F32)
    stats_ref[16:17, 0:heads] = reach
    step = stacked_groups(slot_rows(step_ref[...]))
    logs = column_logs(step, rate_ref, heads)
    scale_ref[...] = jnp.exp(-logs) * step.T
    finals = jnp.exp(logs[Q - 1 : Q, :])
    for group in range(groups):
        start = base + group * Q
        doc_first, next_end = group_bounds(doc_ref, start)
        final = finals[:, group * heads : (group + 1) * heads]
        passing = jnp.where(start + (Q - 1) < next_end, final, 0.0)
        positions = lax.broadcasted_iota(jnp.int32, (N, Q), 1) + start
        b_rows = b_ref[group * Q : (group + 1) * Q, :].astype(F32).T
        tail_ref[group] = jnp.where(positions >= doc_first, b_rows, 0.0).astype(BF16)
        reach = reach * passing
        stats_ref[group : group + 1, 0:heads] = final
        stats_ref[8 + group : 9 + group, 0:heads] = passing
        stats_ref[17 + group : 18 + group, 0:heads] = reach

    def x_of(group, pair):
        if pair == 0:
            wide[group].wait()
        return x_ref[group, :, 2 * pair * P_SIZE : 2 * (pair + 1) * P_SIZE]

    half_states(
        groups,
        half,
        x_of,
        scale_ref,
        lambda group: tail_ref[group],
        stats_ref,
        state_ref,
    )


def own_states_kernel(heads, groups, stats_ref, scale_ref, tail_ref, x_ref, state_ref):
    half_states(
        groups,
        0,
        lambda group, pair: x_ref[group * Q : (group + 1) * Q, head_span(2 * pair, heads, 2)],
        scale_ref,
        lambda group: tail_ref[group],
        stats_ref,
        state_ref,
    )


def inside_kernel(
    heads,
    groups,
    doc_hbm,
    rate_hbm,
    skip_hbm,
    step_hbm,
    b_hbm,
    c_hbm,
    x_hbm,
    gate_hbm,
    after_ref,
    own_u_hbm,
    own_v_hbm,
    away_u_hbm,
    away_v_hbm,
    own_before_hbm,
    away_before_hbm,
    entry_c_hbm,
    token_ref,
    own_u_ref,
    own_v_ref,
    away_u_ref,
    away_v_ref,
    own_before_ref,
    away_before_ref,
    entry_c_ref,
    out_sems,
    doc_ref,
    rate_ref,
    skip_ref,
    step_ref,
    b_ref,
    c_ref,
    x_ref,
    gate_ref,
    small_sems,
    wide_sems,
):
    small = [
        pltpu.make_async_copy(src, dst, small_sems.at[i])
        for i, (src, dst) in enumerate(
            (
                (step_hbm, step_ref),
                (rate_hbm, rate_ref),
                (doc_hbm, doc_ref),
                (skip_hbm, skip_ref),
                (b_hbm, b_ref),
                (c_hbm, c_ref),
            )
        )
    ]
    wide = []
    for group in range(groups):
        for side, (src, dst) in enumerate(((x_hbm, x_ref), (gate_hbm, gate_ref))):
            wide.append(
                pltpu.make_async_copy(
                    src.at[pl.ds(group * Q, Q), :],
                    dst.at[pl.ds(group * Q, Q), :],
                    wide_sems.at[group, side],
                )
            )
    for copy in small + wide:
        copy.start()
    for copy in small:
        copy.wait()
    half = heads // 2
    copies, results = [], []
    base = lax.axis_index("seq") * (groups * Q)
    rows = lax.broadcasted_iota(jnp.int32, (Q, Q), 0)
    cols = lax.broadcasted_iota(jnp.int32, (Q, Q), 1)
    step = stacked_groups(slot_rows(step_ref[...]))
    logs = column_logs(step, rate_ref, heads)
    scales = jnp.exp(-logs) * step.T
    decays = jnp.exp(logs)
    for group in range(groups):
        start = base + group * Q
        block = slice(group * Q, (group + 1) * Q)
        doc_first, next_end = group_bounds(doc_ref, start)
        scale = scales[:, group * heads : (group + 1) * heads]
        decay = decays[:, group * heads : (group + 1) * heads]
        final = decay[Q - 1 : Q, :]
        passing = jnp.where(start + (Q - 1) < next_end, final, 0.0)
        positions = lax.broadcasted_iota(jnp.int32, (Q, N), 0) + start
        entry_c = jnp.where(positions < next_end, c_ref[block, :].astype(F32), 0.0)
        entry_c_ref[block, :] = entry_c.astype(BF16)
        first = jnp.zeros((Q, Q), jnp.int32)
        end = jnp.int32(0)
        for k in range(doc_ref.shape[0]):
            end = end + doc_ref[k]
            first = jnp.where(end - start <= rows, end - start, first)
        scores = lax.dot_general(c_ref[block, :], b_ref[block, :], NT, preferred_element_type=F32)
        masked = jnp.where((cols <= rows) & (cols >= first), scores, 0.0).astype(BF16)
        lanes = lax.broadcasted_iota(jnp.int32, (N, Q), 1) + start
        tail_b = jnp.where(lanes >= doc_first, b_ref[block, :].astype(F32).T, 0.0).astype(BF16)
        wide[2 * group].wait()
        wide[2 * group + 1].wait()
        for pair in range(half):
            x = x_ref[block, head_span(2 * pair, heads, 2)]
            gates = gate_ref[block, head_span(2 * pair, heads, 2)]
            scaled = scaled_pair(x, scale, 2 * pair, heads)
            product = jnp.dot(masked, scaled, preferred_element_type=F32)
            if pair < half // 2:
                u_ref, v_ref, before_ref = own_u_ref, own_v_ref, own_before_ref
            else:
                u_ref, v_ref, before_ref = away_u_ref, away_v_ref, away_before_ref
            if group < groups - 1:
                states = jnp.dot(tail_b, scaled, preferred_element_type=F32)
            for part in range(2):
                slot = 2 * pair + part
                here = slice(part * P_SIZE, (part + 1) * P_SIZE)
                place = slot % half
                span = slice(place * P_SIZE, (place + 1) * P_SIZE)
                gate = 0.5 * gates[:, here].astype(F32)
                active = gate + gate * jnp.tanh(gate)
                carry = head_columns(decay, slot) * active
                direct = skip_ref[head_of(slot, heads)] * x[:, here].astype(F32)
                u_ref[block, span] = product[:, here] * carry + direct * active
                v_ref[block, span] = carry
                if group < groups - 1:
                    state = states[:, here] * final[:, slot : slot + 1]
                    if group > 0:
                        earlier = before_ref[group - 1, place]
                        state = state + earlier * passing[:, slot : slot + 1]
                    before_ref[group, place] = state
            if pair == half // 2 - 1:
                results.append((own_u_ref, own_u_hbm, 0))
                results.append((own_v_ref, own_v_hbm, 1))
                results.append((own_before_ref, own_before_hbm, 2))
            if pair == half - 1:
                results.append((away_u_ref, away_u_hbm, 3))
                results.append((away_v_ref, away_v_hbm, 4))
                results.append((away_before_ref, away_before_hbm, 5))
                results.append((entry_c_ref, entry_c_hbm, 6))
            for src, dst, index in results:
                if len(dst.shape) == 2:
                    where = pl.ds(group * Q, Q)
                elif group < groups - 1:
                    where = group
                else:
                    continue
                copy = pltpu.make_async_copy(
                    src.at[where], dst.at[where], out_sems.at[group, index]
                )
                copy.start()
                copies.append(copy)
            results = []
    for copy in copies:
        copy.wait()
    token_ref[...] = jnp.zeros_like(token_ref)


def join_cores_kernel(
    own_ref, other_ref, joined_hbm, kept_hbm, token_ref, joined_ref, sems
):
    core = core_index()
    half = own_ref.shape[0]
    copies = [pltpu.make_async_copy(other_ref, kept_hbm, sems.at[half])]
    copies[0].start()
    for slot in range(half):
        own, other = own_ref[slot], other_ref[slot]
        earlier = jnp.where(core == 0, own, other)
        later = jnp.where(core == 0, other, own)
        later_pass = later[N : N + 1, :]
        joined_ref[slot, 0:N, :] = later_pass * earlier[0:N, :] + later[0:N, :]
        joined_ref[slot, N : N + 8, :] = later_pass * earlier[N : N + 8, :]
        if slot % 2 == 1:
            part = pl.ds(slot - 1, 2)
            copies.append(
                pltpu.make_async_copy(joined_ref.at[part], joined_hbm.at[part], sems.at[slot])
            )
            copies[-1].start()
    token_ref[...] = jnp.zeros_like(token_ref)
    for copy in copies:
        copy.wait()


def row_total_kernel(parts_ref, inside_ref, swap_ref, total_ref, copy_ref):
    total = parts_ref[0, 0:N, :]
    for chip in range(1, Z_SIZE):
        total = parts_ref[chip, N : N + 1, :] * total + parts_ref[chip, 0:N, :]
    total_ref[...] = total
    copy_ref[...] = parts_ref[...]


def entering_kernel(
    parts_ref,
    other_parts_ref,
    carried_ref,
    other_carried_ref,
    step1_ref,
    step2_ref,
    step3_ref,
    step4_ref,
    here_ref,
    all_ref,
):
    seq = lax.axis_index("seq")
    row = seq // (2 * Z_SIZE)
    z = lax.rem(seq // 2, Z_SIZE)
    core = core_index()
    for which, (chips_ref, before_row_ref) in enumerate(
        ((parts_ref, carried_ref), (other_parts_ref, other_carried_ref))
    ):
        state = jnp.where(row > 0, before_row_ref[...], 0.0)
        for chip in range(Z_SIZE):
            all_ref[which, chip] = state
            if chip < Z_SIZE - 1:
                state = chips_ref[chip, N : N + 1, :] * state + chips_ref[chip, 0:N, :]
    for step, pair_ref in ((0, here_ref), (1, step1_ref), (2, step2_ref), (3, step3_ref)):
        chip = lax.rem(z + jnp.where(core == 0, step, Z_SIZE - step), Z_SIZE)
        pair_ref[0] = all_ref[core, chip]
        pair_ref[1] = all_ref[1 - core, chip]
    step4_ref[0] = all_ref[0, lax.rem(z + 4, Z_SIZE)]


def outputs_kernel(
    heads,
    groups,
    here_ref,
    step1_ref,
    step2_ref,
    step3_ref,
    step4_ref,
    swapped1_ref,
    swapped2_ref,
    swapped3_ref,
    swapped4_ref,
    own_other_ref,
    away_other_ref,
    own_before_ref,
    away_before_ref,
    stats_ref,
    c_ref,
    own_u_ref,
    own_v_ref,
    away_u_ref,
    away_v_ref,
    own_gated_ref,
    away_gated_ref,
    squares_ref,
    first_ref,
):
    core = core_index()
    z = lax.rem(lax.axis_index("seq") // 2, Z_SIZE)
    half = heads // 2

    def place(chip_state, owner, earlier_ref, slot):
        earlier = earlier_ref[owner]
        joined = earlier[N : N + 1, :] * chip_state + earlier[0:N, :]
        first_ref[slot] = jnp.where(core == 0, chip_state, joined)

    up, down = jnp.where(core == 0, 1, Z_SIZE - 1), jnp.where(core == 0, Z_SIZE - 1, 1)
    for pair_ref, distance in (
        (here_ref, 0 * up),
        (step1_ref, down),
        (step2_ref, 2 * down),
        (step3_ref, 3 * down),
        (swapped1_ref, up),
        (swapped2_ref, 2 * up),
        (swapped3_ref, 3 * up),
    ):
        owner = lax.rem(z + distance, Z_SIZE)
        place(pair_ref[0], owner, away_other_ref, owner + core * half)
        place(pair_ref[1], owner, own_other_ref, owner + (1 - core) * half)
    owner = lax.rem(z + 4, Z_SIZE)
    place(step4_ref[0], owner, own_other_ref, owner)
    place(swapped4_ref[0], owner, away_other_ref, half + owner)

    for group in range(groups):
        block = slice(group * Q, (group + 1) * Q)
        reach = stats_ref[16 + group : 17 + group, :]
        squares = jnp.zeros((Q, P_SIZE), F32)
        for side, (u_ref, v_ref, before_ref, gated_ref) in enumerate(
            (
                (own_u_ref, own_v_ref, own_before_ref, own_gated_ref),
                (away_u_ref, away_v_ref, away_before_ref, away_gated_ref),
            )
        ):
            for pair in range(half // 2):
                both = []
                for index in (2 * pair, 2 * pair + 1):
                    slot = side * half + index
                    state = first_ref[slot]
                    if group > 0:
                        state = state * reach[:, slot : slot + 1] + before_ref[group - 1, index]
                    both.append(state.astype(BF16))
                carried = jnp.dot(
                    c_ref[block, :], jnp.concatenate(both, axis=1), preferred_element_type=F32
                )
                span = slice(2 * pair * P_SIZE, 2 * (pair + 1) * P_SIZE)
                gated = u_ref[block, span] + v_ref[block, span] * carried
                gated_ref[block, span] = gated
                square = gated * gated
                squares = squares + square[:, 0:P_SIZE] + square[:, P_SIZE:]
        squares_ref[:, block] = jnp.broadcast_to(
            jnp.sum(squares.T, axis=0, keepdims=True), (8, Q)
        )


def write_states_kernel(
    heads,
    groups,
    first_ref,
    own_before_ref,
    away_before_ref,
    stats_ref,
    after_ref,
    states_hbm,
    token_ref,
    states_ref,
    sems,
):
    half = heads // 2
    copies = []
    for group in range(groups):
        reach = stats_ref[16 + group : 17 + group, :]
        for side, before_ref in enumerate((own_before_ref, away_before_ref)):
            for index in range(half):
                slot = side * half + index
                state = first_ref[slot]
                if group > 0:
                    state = state * reach[:, slot : slot + 1] + before_ref[group - 1, index]
                states_ref[group, side, index] = state.T
            copy = pltpu.make_async_copy(
                states_ref.at[group, side],
                states_hbm.at[group, pl.ds(head_of(side * half, heads), half)],
                sems.at[group, side],
            )
            copy.start()
            copies.append(copy)
    for copy in copies:
        copy.wait()
    token_ref[...] = jnp.zeros_like(token_ref)


SCALE_ROWS = 128


def scale_kernel(
    inner, heads, own_ref, away_ref, gain_ref, sum_ref, a_ref, b_ref, c_ref, after_ref, out_hbm, out_ref, sems
):
    mean = (sum_ref[...] + a_ref[...] + b_ref[...] + c_ref[...]) * (1.0 / inner)
    scale = lax.rsqrt(mean + 1e-05)
    half = heads // 2
    copies = []
    for chunk in range(own_ref.shape[0] // SCALE_ROWS):
        block = slice(chunk * SCALE_ROWS, (chunk + 1) * SCALE_ROWS)
        column = jnp.broadcast_to(scale[0:1, block], (P_SIZE, SCALE_ROWS)).T
        for side, gated_ref in enumerate((own_ref, away_ref)):
            for index in range(half):
                span = slice(index * P_SIZE, (index + 1) * P_SIZE)
                gain = gain_ref[:, head_span(side * half + index, heads)]
                out_ref[side, block, span] = (gated_ref[block, span] * column * gain).astype(BF16)
            copy = pltpu.make_async_copy(
                out_ref.at[side, pl.ds(chunk * SCALE_ROWS, SCALE_ROWS), :],
                out_hbm.at[
                    pl.ds(chunk * SCALE_ROWS, SCALE_ROWS), head_span(side * half, heads, half)
                ],
                sems.at[side, chunk],
            )
            copy.start()
            copies.append(copy)
    for copy in copies:
        copy.wait()


def cost(flops, bytes_accessed):
    return pl.CostEstimate(flops=flops, bytes_accessed=bytes_accessed, transcendentals=0)


def params(mebibytes):
    return pltpu.CompilerParams(vmem_limit_bytes=mebibytes * 1024 * 1024)


def local(
    head_input,
    gate_input,
    step_size,
    input_proj,
    output_proj,
    decay_rate,
    skip_gain,
    norm_gain,
    doc_lengths,
):
    row_count, width = head_input.shape
    heads = step_size.shape[1]
    half = heads // 2
    groups = row_count // Q
    sds = jax.ShapeDtypeStruct
    step_rows = step_size.T
    gain = norm_gain.reshape(1, width)
    smem = pl.BlockSpec(memory_space=pltpu.SMEM)
    vmem = pl.BlockSpec(memory_space=pltpu.VMEM)
    hbm = pl.BlockSpec(memory_space=pltpu.HBM)
    anywhere = pl.BlockSpec(memory_space=pl.ANY)
    dma = pltpu.SemaphoreType.DMA

    token = sds((8, P_SIZE), F32)
    half_state = sds((half, N + 8, P_SIZE), F32)
    half_before = sds((groups - 1, half, N, P_SIZE), F32)
    half_wide = sds((row_count, width // 2), F32)

    def in_hbm(*arrays):
        return [pltpu.with_memory_space_constraint(array, pltpu.HBM) for array in arrays]

    away_state, stats, scale, tail = pl.pallas_call(
        functools.partial(away_states_kernel, heads, groups),
        in_specs=[hbm] * 5,
        out_specs=[vmem] * 4,
        out_shape=[
            half_state,
            sds((24, P_SIZE), F32),
            sds((Q, groups * heads), F32),
            sds((groups, N, Q), BF16),
        ],
        scratch_shapes=[
            pltpu.SMEM(doc_lengths.shape, jnp.int32),
            pltpu.SMEM(decay_rate.shape, F32),
            pltpu.VMEM((heads, row_count), F32),
            pltpu.VMEM((row_count, N), BF16),
            pltpu.VMEM((groups, Q, width // 2), BF16),
            dma((4,)),
            dma((groups,)),
        ],
        compiler_params=params(16),
        cost_estimate=cost(200_000_000, 4_000_000),
        name="away_states",
    )(*in_hbm(doc_lengths, decay_rate, step_rows, input_proj, head_input))
    own_other = lax.ppermute(away_state, "seq", CORE_SWAP)

    own_state = pl.pallas_call(
        functools.partial(own_states_kernel, heads, groups),
        in_specs=[vmem] * 4,
        out_specs=vmem,
        out_shape=half_state,
        compiler_params=params(16),
        cost_estimate=cost(2_000_000_000, 4_000_000),
        name="own_states",
    )(stats, scale, tail, head_input)

    joined, own_kept, joined_token = pl.pallas_call(
        join_cores_kernel,
        in_specs=[vmem, vmem],
        out_specs=[hbm, hbm, vmem],
        out_shape=[pltpu.HBM(half_state.shape, F32)] * 2 + [token],
        scratch_shapes=[pltpu.VMEM(half_state.shape, F32), dma((half + 1,))],
        compiler_params=params(8),
        cost_estimate=cost(1_000_000, 1_700_000),
        name="join_cores",
    )(own_state, own_other)
    parts = lax.all_to_all(
        joined, "seq", split_axis=0, concat_axis=0, axis_index_groups=RINGS, tiled=True
    )
    away_other = lax.ppermute(own_state, "seq", CORE_SWAP)

    own_u, own_v, away_u, away_v, own_before, away_before, entry_c, inside_token = pl.pallas_call(
        functools.partial(inside_kernel, heads, groups),
        in_specs=[hbm] * 8 + [anywhere],
        out_specs=[hbm] * 7 + [vmem],
        out_shape=[pltpu.HBM(half_wide.shape, F32)] * 4
        + [pltpu.HBM(half_before.shape, F32)] * 2
        + [pltpu.HBM((row_count, N), BF16), token],
        scratch_shapes=[pltpu.VMEM(half_wide.shape, F32)] * 4
        + [pltpu.VMEM(half_before.shape, F32)] * 2
        + [pltpu.VMEM((row_count, N), BF16), dma((groups, 7))]
        + [
            pltpu.SMEM(doc_lengths.shape, jnp.int32),
            pltpu.SMEM(decay_rate.shape, F32),
            pltpu.SMEM(skip_gain.shape, F32),
            pltpu.VMEM((heads, row_count), F32),
            pltpu.VMEM((row_count, N), BF16),
            pltpu.VMEM((row_count, N), BF16),
            pltpu.VMEM((row_count, width), BF16),
            pltpu.VMEM((row_count, width), BF16),
            dma((6,)),
            dma((groups, 2)),
        ],
        compiler_params=params(36),
        cost_estimate=cost(8_000_000_000, 20_000_000),
        name="inside",
    )(
        *in_hbm(
            doc_lengths,
            decay_rate,
            skip_gain,
            step_rows,
            input_proj,
            output_proj,
            head_input,
            gate_input,
        ),
        joined_token,
    )
    total, parts = pl.pallas_call(
        row_total_kernel,
        in_specs=[vmem, anywhere, anywhere],
        out_shape=[sds((N, P_SIZE), F32), half_state],
        compiler_params=params(8),
        cost_estimate=cost(300_000, 600_000),
        name="row_total",
    )(parts, inside_token, away_other)
    carried = lax.ppermute(total, "seq", NEXT_ROW)
    other_carried = lax.ppermute(total, "seq", NEXT_ROW_SWAP)
    other_parts = lax.ppermute(parts, "seq", CORE_SWAP)
    pair_state = sds((2, N, P_SIZE), F32)
    *steps, here = pl.pallas_call(
        entering_kernel,
        out_shape=[pair_state] * 3 + [sds((1, N, P_SIZE), F32), pair_state],
        scratch_shapes=[pltpu.VMEM((2, Z_SIZE, N, P_SIZE), F32)],
        compiler_params=params(8),
        cost_estimate=cost(20_000_000_000, 1_100_000),
        name="entering",
    )(parts, other_parts, carried, other_carried)
    arrived = [lax.ppermute(sent, "seq", pairs) for sent, pairs in zip(steps, AROUND)]
    swapped = [lax.ppermute(state, "seq", CORE_SWAP) for state in arrived]

    own_gated, away_gated, squares, first = pl.pallas_call(
        functools.partial(outputs_kernel, heads, groups),
        in_specs=[vmem] * 19,
        out_specs=[vmem] * 4,
        out_shape=[half_wide] * 2 + [sds((8, row_count), F32), sds((heads, N, P_SIZE), F32)],
        compiler_params=params(30),
        cost_estimate=cost(2_000_000, 9_000),
        name="outputs",
    )(
        here,
        *arrived,
        *swapped,
        own_kept,
        away_other,
        own_before,
        away_before,
        stats,
        entry_c,
        own_u,
        own_v,
        away_u,
        away_v,
    )

    tp_size = 4
    sums = [
        lax.ppermute(squares, "tp", [(i, (i + k) % tp_size) for i in range(tp_size)])
        for k in range(1, tp_size)
    ]
    group_states, states_token = pl.pallas_call(
        functools.partial(write_states_kernel, heads, groups),
        in_specs=[vmem] * 4 + [anywhere],
        out_specs=[hbm, vmem],
        out_shape=[sds((groups, heads, P_SIZE, N), F32), token],
        scratch_shapes=[
            pltpu.VMEM((groups, 2, half, P_SIZE, N), F32),
            dma((groups, 2)),
        ],
        compiler_params=params(16),
        cost_estimate=cost(4_000_000_000, 9_000_000),
        name="write_states",
    )(first, own_before, away_before, stats, squares)
    mixed_out = pl.pallas_call(
        functools.partial(scale_kernel, width * tp_size, heads),
        in_specs=[vmem] * 7 + [anywhere],
        out_specs=hbm,
        out_shape=sds((row_count, width), BF16),
        scratch_shapes=[
            pltpu.VMEM((2, row_count, width // 2), BF16),
            dma((2, row_count // SCALE_ROWS)),
        ],
        compiler_params=params(16),
        cost_estimate=cost(5_000_000, 6_500_000),
        name="scale",
    )(own_gated, away_gated, gain, squares, *sums, states_token)
    return (mixed_out, group_states)


def solution(mesh):
    return jax.shard_map(
        local,
        mesh=mesh,
        in_specs=(
            P("seq", "tp"),
            P("seq", "tp"),
            P("seq", "tp"),
            P("seq", None),
            P("seq", None),
            P("tp"),
            P("tp"),
            P("tp"),
            P(),
        ),
        out_specs=(P("seq", "tp"), P("seq", "tp", None, None)),
        check_vma=False,
    )
```

```python
import functools
import jax
import jax.numpy as jnp
from jax import lax
from jax.experimental import pallas as pl
from jax.experimental.pallas import tpu as pltpu
from jax.sharding import PartitionSpec as P

P_SIZE = 128
N = 128
Q = 256
F32 = jnp.float32
BF16 = jnp.bfloat16
Y_SIZE = 4
Z_SIZE = 8
NT = (((1,), (1,)), ((), ()))


def seq_index(y, z, core):
    return ((y % Y_SIZE) * Z_SIZE + (z % Z_SIZE)) * 2 + core


def seq_pairs(move):
    pairs = []
    for y in range(Y_SIZE):
        for z in range(Z_SIZE):
            for core in range(2):
                pairs.append((seq_index(y, z, core), seq_index(*move(y, z, core))))
    return pairs


CORE_SWAP = seq_pairs(lambda y, z, core: (y, z, 1 - core))
NEXT_ROW = seq_pairs(lambda y, z, core: (y + 1, z, core))
AROUND = [
    seq_pairs(lambda y, z, core, step=step: (y, z + (step if core == 0 else -step), core))
    for step in range(1, 5)
]


def group_bounds(doc_ref, start):
    last = start + (Q - 1)
    doc_first = jnp.int32(0)
    next_end = jnp.int32(2147483647)
    end = jnp.int32(0)
    for k in range(doc_ref.shape[0]):
        end = end + doc_ref[k]
        doc_first = jnp.where(end <= last, end, doc_first)
        next_end = jnp.minimum(next_end, jnp.where(end >= start, end, 2147483647))
    return doc_first, next_end


def split3(values):
    high = values.astype(BF16)
    rest = values - high.astype(F32)
    mid = rest.astype(BF16)
    low = (rest - mid.astype(F32)).astype(BF16)
    return high, mid, low


def core_index():
    return lax.axis_index("seq") & 1


def ring_index():
    return (lax.axis_index("seq") // 2) & (Z_SIZE - 1)


def chip_at(core, step):
    return (ring_index() + jnp.where(core == 0, step, Z_SIZE - step)) & (Z_SIZE - 1)


def head_of(slot, heads):
    half = heads // 2
    core = core_index() if slot < half else 1 - core_index()
    place = slot % half
    if place < 6:
        return chip_at(core, place // 2 + 1) + half * (place % 2)
    return core * half + chip_at(core, 4 if place == 6 else 0)


def head_spans(heads):
    return [
        pl.ds(pl.multiple_of(head_of(slot, heads) * P_SIZE, P_SIZE), P_SIZE)
        for slot in range(heads)
    ]


def slot_rows(rows_ref):
    heads = rows_ref.shape[0]
    return jnp.concatenate(
        [rows_ref[pl.ds(head_of(slot, heads), 1), :] for slot in range(heads)], axis=0
    )


def stacked_groups(rows):
    groups = rows.shape[1] // Q
    return jnp.concatenate([rows[:, g * Q : (g + 1) * Q] for g in range(groups)], axis=0)


def column_logs(step, rate_ref, heads):
    head_rows = lax.rem(lax.broadcasted_iota(jnp.int32, step.shape, 0), heads)
    rates = jnp.zeros_like(step)
    for slot in range(heads):
        rates = jnp.where(head_rows == slot, -rate_ref[head_of(slot, heads)], rates)
    rows = lax.broadcasted_iota(jnp.int32, (Q, Q), 0)
    cols = lax.broadcasted_iota(jnp.int32, (Q, Q), 1)
    lower = jnp.where(cols <= rows, 1.0, 0.0).astype(BF16)
    return sum(
        lax.dot_general(lower, part, NT, preferred_element_type=F32)
        for part in split3(rates * step)
    )


def head_columns(values, head):
    return jnp.broadcast_to(values[:, head : head + 1], (values.shape[0], P_SIZE))


def scaled_pair(columns, scale, slot):
    parts = [
        (columns[part].astype(F32) * head_columns(scale, slot + part)).astype(BF16)
        for part in range(2)
    ]
    return jnp.concatenate(parts, axis=1)


def half_states(groups, first_slot, x_ref, scale_ref, tail_of, stats_ref, state_ref, ready):
    half = state_ref.shape[0]
    spans = head_spans(2 * half)
    for group in range(groups):
        final = stats_ref[group : group + 1, :]
        passing = stats_ref[8 + group : 9 + group, :]
        tail_b = tail_of(group)
        ready(group)
        block = slice(group * Q, (group + 1) * Q)
        scale = scale_ref[:, group * 2 * half : (group + 1) * 2 * half]
        for pair in range(half // 2):
            slot = first_slot + 2 * pair
            columns = [x_ref[block, spans[slot + part]] for part in range(2)]
            scaled = scaled_pair(columns, scale, slot)
            product = jnp.dot(tail_b, scaled, preferred_element_type=F32)
            for part in range(2):
                lane = slice(slot + part, slot + part + 1)
                index = 2 * pair + part
                state = product[:, part * P_SIZE : (part + 1) * P_SIZE] * final[:, lane]
                if group > 0:
                    state = state + state_ref[index, 0:N, :] * passing[:, lane]
                state_ref[index, 0:N, :] = state
    reach = stats_ref[16 + groups : 17 + groups, :]
    for index in range(half):
        lane = slice(first_slot + index, first_slot + index + 1)
        state_ref[index, N : N + 8, :] = jnp.broadcast_to(reach[:, lane], (8, P_SIZE))


def away_states_kernel(
    heads,
    groups,
    doc_hbm,
    rate_hbm,
    step_hbm,
    b_hbm,
    x_hbm,
    state_ref,
    stats_ref,
    scale_ref,
    tail_ref,
    logs_ref,
    x_ref,
    doc_ref,
    rate_ref,
    step_ref,
    b_ref,
    small_sems,
    wide_sems,
):
    half = heads // 2
    small = [
        pltpu.make_async_copy(src, dst, small_sems.at[i])
        for i, (src, dst) in enumerate(
            ((step_hbm, step_ref), (rate_hbm, rate_ref), (doc_hbm, doc_ref), (b_hbm, b_ref))
        )
    ]
    wide = [
        pltpu.make_async_copy(
            x_hbm.at[pl.ds(group * Q, Q), :],
            x_ref.at[pl.ds(group * Q, Q), :],
            wide_sems.at[group],
        )
        for group in range(groups)
    ]
    for copy in small + wide:
        copy.start()
    for copy in small:
        copy.wait()
    stats_ref[...] = jnp.zeros_like(stats_ref)
    base = lax.axis_index("seq") * (groups * Q)
    reach = jnp.ones((1, heads), F32)
    stats_ref[16:17, 0:heads] = reach
    step = stacked_groups(slot_rows(step_ref))
    logs = column_logs(step, rate_ref, heads)
    logs_ref[...] = logs
    scale_ref[...] = jnp.exp(-logs) * step.T
    finals = jnp.exp(logs[Q - 1 : Q, :])
    for group in range(groups):
        start = base + group * Q
        doc_first, next_end = group_bounds(doc_ref, start)
        final = finals[:, group * heads : (group + 1) * heads]
        passing = jnp.where(start + (Q - 1) < next_end, final, 0.0)
        positions = lax.broadcasted_iota(jnp.int32, (N, Q), 1) + start
        b_rows = b_ref[group * Q : (group + 1) * Q, :].astype(F32).T
        tail_ref[group] = jnp.where(positions >= doc_first, b_rows, 0.0).astype(BF16)
        reach = reach * passing
        stats_ref[group : group + 1, 0:heads] = final
        stats_ref[8 + group : 9 + group, 0:heads] = passing
        stats_ref[17 + group : 18 + group, 0:heads] = reach

    half_states(
        groups,
        half,
        x_ref,
        scale_ref,
        lambda group: tail_ref[group],
        stats_ref,
        state_ref,
        lambda group: wide[group].wait(),
    )


def own_states_kernel(heads, groups, stats_ref, scale_ref, tail_ref, x_ref, state_ref):
    half_states(
        groups,
        0,
        x_ref,
        scale_ref,
        lambda group: tail_ref[group],
        stats_ref,
        state_ref,
        lambda group: None,
    )


def half_inside(
    heads,
    groups,
    first_slot,
    skip_ref,
    stats_ref,
    scale_ref,
    tail_ref,
    decay_ref,
    masked_ref,
    x_ref,
    gate_ref,
    u_ref,
    v_ref,
    before_ref,
):
    half = heads // 2
    spans = head_spans(heads)
    skips = [skip_ref[head_of(first_slot + place, heads)] for place in range(half)]
    for group in range(groups):
        block = slice(group * Q, (group + 1) * Q)
        lanes = slice(group * heads, (group + 1) * heads)
        scale = scale_ref[:, lanes]
        decay = decay_ref[:, lanes]
        final = stats_ref[group : group + 1, :]
        passing = stats_ref[8 + group : 9 + group, :]
        masked = masked_ref[group]
        for pair in range(half // 2):
            slot = first_slot + 2 * pair
            columns = [x_ref[block, spans[slot + part]] for part in range(2)]
            scaled = scaled_pair(columns, scale, slot)
            product = jnp.dot(masked, scaled, preferred_element_type=F32)
            if group < groups - 1:
                states = jnp.dot(tail_ref[group], scaled, preferred_element_type=F32)
            for part in range(2):
                here = slice(part * P_SIZE, (part + 1) * P_SIZE)
                place = 2 * pair + part
                span = slice(place * P_SIZE, (place + 1) * P_SIZE)
                gate = 0.5 * gate_ref[block, spans[slot + part]].astype(F32)
                active = gate + gate * jnp.tanh(gate)
                carry = head_columns(decay, slot + part) * active
                direct = skips[place] * columns[part].astype(F32)
                u_ref[block, span] = product[:, here] * carry + direct * active
                v_ref[block, span] = carry
                if group < groups - 1:
                    lane = slice(slot + part, slot + part + 1)
                    state = states[:, here] * final[:, lane]
                    if group > 0:
                        state = state + before_ref[group - 1, place] * passing[:, lane]
                    before_ref[group, place] = state


def away_inside_kernel(
    heads,
    groups,
    doc_ref,
    skip_ref,
    logs_ref,
    b_ref,
    c_ref,
    stats_ref,
    scale_ref,
    tail_ref,
    x_ref,
    gate_ref,
    after_ref,
    u_ref,
    v_ref,
    before_ref,
    entry_c_ref,
    decay_ref,
    masked_ref,
    token_ref,
):
    base = lax.axis_index("seq") * (groups * Q)
    rows = lax.broadcasted_iota(jnp.int32, (Q, Q), 0)
    cols = lax.broadcasted_iota(jnp.int32, (Q, Q), 1)
    decay_ref[...] = jnp.exp(logs_ref[...])
    for group in range(groups):
        start = base + group * Q
        block = slice(group * Q, (group + 1) * Q)
        _, next_end = group_bounds(doc_ref, start)
        positions = lax.broadcasted_iota(jnp.int32, (Q, N), 0) + start
        entry_c = jnp.where(positions < next_end, c_ref[block, :].astype(F32), 0.0)
        entry_c_ref[block, :] = entry_c.astype(BF16)
        first = jnp.zeros((Q, Q), jnp.int32)
        end = jnp.int32(0)
        for k in range(doc_ref.shape[0]):
            end = end + doc_ref[k]
            first = jnp.where(end - start <= rows, end - start, first)
        scores = lax.dot_general(c_ref[block, :], b_ref[block, :], NT, preferred_element_type=F32)
        masked = jnp.where((cols <= rows) & (cols >= first), scores, 0.0)
        masked_ref[group] = masked.astype(BF16)
    half_inside(
        heads,
        groups,
        heads // 2,
        skip_ref,
        stats_ref,
        scale_ref,
        tail_ref,
        decay_ref,
        masked_ref,
        x_ref,
        gate_ref,
        u_ref,
        v_ref,
        before_ref,
    )
    token_ref[...] = jnp.zeros_like(token_ref)


def own_inside_kernel(
    heads,
    groups,
    skip_ref,
    stats_ref,
    scale_ref,
    tail_ref,
    decay_ref,
    masked_ref,
    x_ref,
    gate_ref,
    after_ref,
    u_ref,
    v_ref,
    before_ref,
    token_ref,
):
    half_inside(
        heads,
        groups,
        0,
        skip_ref,
        stats_ref,
        scale_ref,
        tail_ref,
        decay_ref,
        masked_ref,
        x_ref,
        gate_ref,
        u_ref,
        v_ref,
        before_ref,
    )
    token_ref[...] = jnp.zeros_like(token_ref)


def join_cores_kernel(
    own_ref, other_ref, step1_ref, step2_ref, step3_ref, step4_ref, here_ref, token_ref
):
    core = core_index()
    places = [(ref, part) for ref in (step1_ref, step2_ref, step3_ref) for part in range(2)]
    for slot, (joined_ref, part) in enumerate(places + [(step4_ref, 0), (here_ref, 0)]):
        own, other = own_ref[slot], other_ref[slot]
        earlier = jnp.where(core == 0, own, other)
        later = jnp.where(core == 0, other, own)
        later_pass = later[N : N + 1, :]
        joined_ref[part, 0:N, :] = later_pass * earlier[0:N, :] + later[0:N, :]
        joined_ref[part, N : N + 8, :] = later_pass * earlier[N : N + 8, :]
    token_ref[...] = jnp.zeros_like(token_ref)


def pack_kernel(step1_ref, step2_ref, step3_ref, step4_ref, last_ref, after_ref, packed_ref):
    for step, ref in enumerate((step1_ref, step2_ref, step3_ref)):
        packed_ref[2 * step] = ref[0]
        packed_ref[2 * step + 1] = ref[1]
    packed_ref[6] = step4_ref[0]
    packed_ref[7] = last_ref[0]


def row_total_kernel(packed_ref, swapped_ref, after_ref, total_ref, parts_ref):
    core = core_index()
    for ref, arrived_on in ((packed_ref, core), (swapped_ref, 1 - core)):
        for step in (1, 2, 3):
            chip = chip_at(1 - arrived_on, step)
            parts_ref[0, chip] = ref[2 * step - 2]
            parts_ref[1, chip] = ref[2 * step - 1]
        parts_ref[arrived_on, chip_at(core, 4)] = ref[6]
        parts_ref[arrived_on, chip_at(core, 0)] = ref[7]
    for which in range(2):
        total = parts_ref[which, 0, 0:N, :]
        for chip in range(1, Z_SIZE):
            total = parts_ref[which, chip, N : N + 1, :] * total + parts_ref[which, chip, 0:N, :]
        total_ref[which] = total


def entering_kernel(
    parts_ref,
    carried_ref,
    step1_ref,
    step2_ref,
    step3_ref,
    step4_ref,
    here_ref,
    token_ref,
    all_ref,
):
    row = lax.axis_index("seq") // (2 * Z_SIZE)
    core = core_index()
    for which in range(2):
        state = jnp.where(row > 0, carried_ref[which], 0.0)
        for chip in range(Z_SIZE):
            all_ref[which, chip] = state
            if chip < Z_SIZE - 1:
                state = parts_ref[which, chip, N : N + 1, :] * state + parts_ref[which, chip, 0:N, :]
    for step, pair_ref in ((1, step1_ref), (2, step2_ref), (3, step3_ref)):
        chip = chip_at(core, step)
        pair_ref[0] = all_ref[0, chip]
        pair_ref[1] = all_ref[1, chip]
    step4_ref[0] = all_ref[core, chip_at(core, 4)]
    here_ref[0] = all_ref[core, chip_at(core, 0)]
    here_ref[1] = all_ref[1 - core, chip_at(core, 0)]
    token_ref[...] = jnp.zeros_like(token_ref)


def outputs_kernel(
    heads,
    groups,
    here_ref,
    packed_ref,
    swapped_ref,
    own_other_ref,
    away_other_ref,
    own_before_ref,
    away_before_ref,
    stats_ref,
    c_ref,
    own_u_ref,
    own_v_ref,
    away_u_ref,
    away_v_ref,
    own_gated_ref,
    away_gated_ref,
    squares_ref,
    first_ref,
):
    core = core_index()
    half = heads // 2
    for side, earlier_ref in enumerate((own_other_ref, away_other_ref)):
        for place in range(half):
            if place < 6:
                chip_state = (swapped_ref, packed_ref)[side][place]
            elif place == 6:
                chip_state = (packed_ref, swapped_ref)[side][place]
            else:
                chip_state = here_ref[side]
            joined = earlier_ref[place, N : N + 1, :] * chip_state + earlier_ref[place, 0:N, :]
            first_ref[side * half + place] = jnp.where(core == 0, chip_state, joined)

    for group in range(groups):
        block = slice(group * Q, (group + 1) * Q)
        reach = stats_ref[16 + group : 17 + group, :]
        squares = jnp.zeros((Q, P_SIZE), F32)
        for side, (u_ref, v_ref, before_ref, gated_ref) in enumerate(
            (
                (own_u_ref, own_v_ref, own_before_ref, own_gated_ref),
                (away_u_ref, away_v_ref, away_before_ref, away_gated_ref),
            )
        ):
            for pair in range(half // 2):
                both = []
                for index in (2 * pair, 2 * pair + 1):
                    slot = side * half + index
                    state = first_ref[slot]
                    if group > 0:
                        state = state * reach[:, slot : slot + 1] + before_ref[group - 1, index]
                    both.append(state.astype(BF16))
                carried = jnp.dot(
                    c_ref[block, :], jnp.concatenate(both, axis=1), preferred_element_type=F32
                )
                span = slice(2 * pair * P_SIZE, 2 * (pair + 1) * P_SIZE)
                gated = u_ref[block, span] + v_ref[block, span] * carried
                gated_ref[block, span] = gated
                square = gated * gated
                squares = squares + square[:, 0:P_SIZE] + square[:, P_SIZE:]
        squares_ref[:, block] = jnp.broadcast_to(
            jnp.sum(squares.T, axis=0, keepdims=True), (8, Q)
        )


def write_states_kernel(
    heads,
    groups,
    first_ref,
    own_before_ref,
    away_before_ref,
    stats_ref,
    after_ref,
    states_hbm,
    token_ref,
    states_ref,
    sems,
):
    half = heads // 2
    copies = []
    places = [head_of(slot, heads) for slot in range(heads)]
    for group in range(groups):
        reach = stats_ref[16 + group : 17 + group, :]
        for side, before_ref in enumerate((own_before_ref, away_before_ref)):
            for index in range(half):
                slot = side * half + index
                state = first_ref[slot]
                if group > 0:
                    state = state * reach[:, slot : slot + 1] + before_ref[group - 1, index]
                states_ref[group, slot] = state.T
                copy = pltpu.make_async_copy(
                    states_ref.at[group, slot],
                    states_hbm.at[group, places[slot]],
                    sems.at[group, slot],
                )
                copy.start()
                copies.append(copy)
    for copy in copies:
        copy.wait()
    token_ref[...] = jnp.zeros_like(token_ref)


SCALE_ROWS = 128


def scale_kernel(
    inner, heads, own_ref, away_ref, gain_ref, sum_ref, a_ref, b_ref, c_ref, after_ref, out_hbm, out_ref, sems
):
    mean = (sum_ref[...] + a_ref[...] + b_ref[...] + c_ref[...]) * (1.0 / inner)
    scale = lax.rsqrt(mean + 1e-05)
    half = heads // 2
    spans = head_spans(heads)
    copies = []
    for chunk in range(own_ref.shape[0] // SCALE_ROWS):
        block = slice(chunk * SCALE_ROWS, (chunk + 1) * SCALE_ROWS)
        column = jnp.broadcast_to(scale[0:1, block], (P_SIZE, SCALE_ROWS)).T
        for slot in range(heads):
            gated_ref = own_ref if slot < half else away_ref
            span = slice(slot % half * P_SIZE, (slot % half + 1) * P_SIZE)
            place = spans[slot]
            out_ref[block, place] = (
                gated_ref[block, span] * column * gain_ref[:, place]
            ).astype(BF16)
        rows = pl.ds(chunk * SCALE_ROWS, SCALE_ROWS)
        copy = pltpu.make_async_copy(
            out_ref.at[rows, :], out_hbm.at[rows, :], sems.at[chunk]
        )
        copy.start()
        copies.append(copy)
    for copy in copies:
        copy.wait()


def cost(flops, bytes_accessed):
    return pl.CostEstimate(flops=flops, bytes_accessed=bytes_accessed, transcendentals=0)


def params(mebibytes):
    return pltpu.CompilerParams(vmem_limit_bytes=mebibytes * 1024 * 1024)


def local(
    head_input,
    gate_input,
    step_size,
    input_proj,
    output_proj,
    decay_rate,
    skip_gain,
    norm_gain,
    doc_lengths,
):
    row_count, width = head_input.shape
    heads = step_size.shape[1]
    half = heads // 2
    groups = row_count // Q
    sds = jax.ShapeDtypeStruct
    step_rows = step_size.T
    gain = norm_gain.reshape(1, width)
    smem = pl.BlockSpec(memory_space=pltpu.SMEM)
    vmem = pl.BlockSpec(memory_space=pltpu.VMEM)
    hbm = pl.BlockSpec(memory_space=pltpu.HBM)
    anywhere = pl.BlockSpec(memory_space=pl.ANY)
    dma = pltpu.SemaphoreType.DMA

    token = sds((8, P_SIZE), F32)
    half_state = sds((half, N + 8, P_SIZE), F32)
    half_before = sds((groups - 1, half, N, P_SIZE), F32)
    half_wide = sds((row_count, width // 2), F32)

    def in_hbm(*arrays):
        return [pltpu.with_memory_space_constraint(array, pltpu.HBM) for array in arrays]

    pair_state = sds((2, N + 8, P_SIZE), F32)
    one_state = sds((1, N + 8, P_SIZE), F32)
    pair_first = sds((2, N, P_SIZE), F32)
    one_first = sds((1, N, P_SIZE), F32)
    lanes = groups * heads

    away_state, stats, scale, tail, logs, input_copy = pl.pallas_call(
        functools.partial(away_states_kernel, heads, groups),
        in_specs=[hbm] * 5,
        out_specs=[vmem] * 6,
        out_shape=[
            half_state,
            sds((24, P_SIZE), F32),
            sds((Q, lanes), F32),
            sds((groups, N, Q), BF16),
            sds((Q, lanes), F32),
            sds((row_count, width), BF16),
        ],
        scratch_shapes=[
            pltpu.SMEM(doc_lengths.shape, jnp.int32),
            pltpu.SMEM(decay_rate.shape, F32),
            pltpu.VMEM((heads, row_count), F32),
            pltpu.VMEM((row_count, N), BF16),
            dma((4,)),
            dma((groups,)),
        ],
        compiler_params=params(16),
        cost_estimate=cost(200_000_000, 4_000_000),
        name="away_states",
    )(*in_hbm(doc_lengths, decay_rate, step_rows, input_proj, head_input))
    own_other = lax.ppermute(away_state, "seq", CORE_SWAP)

    own_state = pl.pallas_call(
        functools.partial(own_states_kernel, heads, groups),
        in_specs=[vmem] * 4,
        out_specs=vmem,
        out_shape=half_state,
        compiler_params=params(16),
        cost_estimate=cost(2_000_000_000, 4_000_000),
        name="own_states",
    )(stats, scale, tail, input_copy)

    *joined, joined_token = pl.pallas_call(
        join_cores_kernel,
        out_shape=[pair_state] * 3 + [one_state] * 2 + [token],
        compiler_params=params(8),
        cost_estimate=cost(1_000_000, 1_700_000),
        name="join_cores",
    )(own_state, own_other)
    here_part = joined.pop()
    arrived = [lax.ppermute(sent, "seq", pairs) for sent, pairs in zip(joined, AROUND)]
    away_other = lax.ppermute(own_state, "seq", CORE_SWAP)

    away_u, away_v, away_before, entry_c, decay, masked, away_token = pl.pallas_call(
        functools.partial(away_inside_kernel, heads, groups),
        in_specs=[smem] * 2 + [vmem] * 8 + [anywhere],
        out_specs=[vmem] * 7,
        out_shape=[half_wide] * 2
        + [
            half_before,
            sds((row_count, N), BF16),
            sds((Q, lanes), F32),
            sds((groups, Q, Q), BF16),
            token,
        ],
        compiler_params=params(24),
        cost_estimate=cost(8_000_000_000, 20_000_000),
        name="away_inside",
    )(
        doc_lengths,
        skip_gain,
        logs,
        input_proj,
        output_proj,
        stats,
        scale,
        tail,
        input_copy,
        gate_input,
        joined_token,
    )

    def pack(states, last, after, name):
        return pl.pallas_call(
            pack_kernel,
            in_specs=[vmem] * 5 + [anywhere],
            out_specs=vmem,
            out_shape=sds((8,) + last.shape[1:], F32),
            compiler_params=params(8),
            cost_estimate=cost(300_000, 1_100_000),
            name=name,
        )(*states, last, after)

    packed_parts = pack(arrived, here_part, away_token, "pack_parts")
    swapped_parts = lax.ppermute(packed_parts, "seq", CORE_SWAP)
    total, parts = pl.pallas_call(
        row_total_kernel,
        in_specs=[vmem, vmem, anywhere],
        out_shape=[pair_first, sds((2, Z_SIZE, N + 8, P_SIZE), F32)],
        compiler_params=params(8),
        cost_estimate=cost(300_000, 600_000),
        name="row_total",
    )(packed_parts, swapped_parts, away_other)
    carried = lax.ppermute(total, "seq", NEXT_ROW)
    *steps, here, entering_token = pl.pallas_call(
        entering_kernel,
        out_shape=[pair_first] * 3 + [one_first, pair_first, token],
        scratch_shapes=[pltpu.VMEM((2, Z_SIZE, N, P_SIZE), F32)],
        compiler_params=params(8),
        cost_estimate=cost(1_000_000, 1_100_000),
        name="entering",
    )(parts, carried)
    returned = [lax.ppermute(sent, "seq", pairs) for sent, pairs in zip(steps, AROUND)]

    own_u, own_v, own_before, own_token = pl.pallas_call(
        functools.partial(own_inside_kernel, heads, groups),
        in_specs=[smem] + [vmem] * 7 + [anywhere],
        out_specs=[vmem] * 4,
        out_shape=[half_wide] * 2 + [half_before, token],
        compiler_params=params(20),
        cost_estimate=cost(8_000_000_000, 20_000_000),
        name="own_inside",
    )(skip_gain, stats, scale, tail, decay, masked, input_copy, gate_input, entering_token)
    packed = pack(returned, here, own_token, "pack_states")
    swapped = lax.ppermute(packed, "seq", CORE_SWAP)

    own_gated, away_gated, squares, first = pl.pallas_call(
        functools.partial(outputs_kernel, heads, groups),
        in_specs=[vmem] * 13,
        out_specs=[vmem] * 4,
        out_shape=[half_wide] * 2 + [sds((8, row_count), F32), sds((heads, N, P_SIZE), F32)],
        compiler_params=params(30),
        cost_estimate=cost(2_000_000, 9_000),
        name="outputs",
    )(
        here,
        packed,
        swapped,
        own_other,
        away_other,
        own_before,
        away_before,
        stats,
        entry_c,
        own_u,
        own_v,
        away_u,
        away_v,
    )

    tp_size = 4
    sums = [
        lax.ppermute(squares, "tp", [(i, (i + k) % tp_size) for i in range(tp_size)])
        for k in range(1, tp_size)
    ]
    group_states, states_token = pl.pallas_call(
        functools.partial(write_states_kernel, heads, groups),
        in_specs=[vmem] * 4 + [anywhere],
        out_specs=[hbm, vmem],
        out_shape=[sds((groups, heads, P_SIZE, N), F32), token],
        scratch_shapes=[
            pltpu.VMEM((groups, heads, P_SIZE, N), F32),
            dma((groups, heads)),
        ],
        compiler_params=params(16),
        cost_estimate=cost(4_000_000_000, 9_000_000),
        name="write_states",
    )(first, own_before, away_before, stats, squares)
    mixed_out = pl.pallas_call(
        functools.partial(scale_kernel, width * tp_size, heads),
        in_specs=[vmem] * 7 + [anywhere],
        out_specs=hbm,
        out_shape=sds((row_count, width), BF16),
        scratch_shapes=[
            pltpu.VMEM((row_count, width), BF16),
            dma((row_count // SCALE_ROWS,)),
        ],
        compiler_params=params(16),
        cost_estimate=cost(5_000_000, 6_500_000),
        name="scale",
    )(own_gated, away_gated, gain, squares, *sums, states_token)
    return (mixed_out, group_states)


def solution(mesh):
    return jax.shard_map(
        local,
        mesh=mesh,
        in_specs=(
            P("seq", "tp"),
            P("seq", "tp"),
            P("seq", "tp"),
            P("seq", None),
            P("seq", None),
            P("tp"),
            P("tp"),
            P("tp"),
            P(),
        ),
        out_specs=(P("seq", "tp"), P("seq", "tp", None, None)),
        check_vma=False,
    )
```

```python
import functools
import jax
import jax.numpy as jnp
from jax import lax
from jax.experimental import pallas as pl
from jax.experimental.pallas import tpu as pltpu
from jax.sharding import PartitionSpec as P

P_SIZE = 128
N = 128
Q = 256
F32 = jnp.float32
BF16 = jnp.bfloat16
Y_SIZE = 4
Z_SIZE = 8
NT = (((1,), (1,)), ((), ()))


def seq_index(y, z, core):
    return ((y % Y_SIZE) * Z_SIZE + (z % Z_SIZE)) * 2 + core


def seq_pairs(move):
    pairs = []
    for y in range(Y_SIZE):
        for z in range(Z_SIZE):
            for core in range(2):
                pairs.append((seq_index(y, z, core), seq_index(*move(y, z, core))))
    return pairs


CORE_SWAP = seq_pairs(lambda y, z, core: (y, z, 1 - core))
NEXT_ROW = seq_pairs(lambda y, z, core: (y + 1, z, core))
AROUND = [
    seq_pairs(lambda y, z, core, step=step: (y, z + (step if core == 0 else -step), core))
    for step in range(1, 5)
]


def group_bounds(doc_ref, start):
    last = start + (Q - 1)
    doc_first = jnp.int32(0)
    next_end = jnp.int32(2147483647)
    end = jnp.int32(0)
    for k in range(doc_ref.shape[0]):
        end = end + doc_ref[k]
        doc_first = jnp.where(end <= last, end, doc_first)
        next_end = jnp.minimum(next_end, jnp.where(end >= start, end, 2147483647))
    return doc_first, next_end


def split3(values):
    high = values.astype(BF16)
    rest = values - high.astype(F32)
    mid = rest.astype(BF16)
    low = (rest - mid.astype(F32)).astype(BF16)
    return high, mid, low


def core_index():
    return lax.axis_index("seq") & 1


def ring_index():
    return (lax.axis_index("seq") // 2) & (Z_SIZE - 1)


def chip_at(core, step):
    return (ring_index() + jnp.where(core == 0, step, Z_SIZE - step)) & (Z_SIZE - 1)


def head_of(slot, heads):
    half = heads // 2
    core = core_index() if slot < half else 1 - core_index()
    place = slot % half
    if place < 6:
        return chip_at(core, place // 2 + 1) + half * (place % 2)
    return core * half + chip_at(core, 4 if place == 6 else 0)


def head_spans(heads):
    return [
        pl.ds(pl.multiple_of(head_of(slot, heads) * P_SIZE, P_SIZE), P_SIZE)
        for slot in range(heads)
    ]


def slot_rows(rows_ref):
    heads = rows_ref.shape[0]
    return jnp.concatenate(
        [rows_ref[pl.ds(head_of(slot, heads), 1), :] for slot in range(heads)], axis=0
    )


def stacked_groups(rows):
    groups = rows.shape[1] // Q
    return jnp.concatenate([rows[:, g * Q : (g + 1) * Q] for g in range(groups)], axis=0)


def column_logs(step, rate_ref, heads):
    head_rows = lax.rem(lax.broadcasted_iota(jnp.int32, step.shape, 0), heads)
    rates = jnp.zeros_like(step)
    for slot in range(heads):
        rates = jnp.where(head_rows == slot, -rate_ref[head_of(slot, heads)], rates)
    rows = lax.broadcasted_iota(jnp.int32, (Q, Q), 0)
    cols = lax.broadcasted_iota(jnp.int32, (Q, Q), 1)
    lower = jnp.where(cols <= rows, 1.0, 0.0).astype(BF16)
    return sum(
        lax.dot_general(lower, part, NT, preferred_element_type=F32)
        for part in split3(rates * step)
    )


def head_columns(values, head):
    return jnp.broadcast_to(values[:, head : head + 1], (values.shape[0], P_SIZE))


def scaled_pair(columns, scale, slot):
    parts = [
        (columns[part].astype(F32) * head_columns(scale, slot + part)).astype(BF16)
        for part in range(2)
    ]
    return jnp.concatenate(parts, axis=1)


def half_states(groups, first_slot, x_ref, scale_ref, tail_of, stats_ref, state_ref, ready):
    half = state_ref.shape[0]
    spans = head_spans(2 * half)
    for group in range(groups):
        final = stats_ref[group : group + 1, :]
        passing = stats_ref[8 + group : 9 + group, :]
        tail_b = tail_of(group)
        ready(group)
        block = slice(group * Q, (group + 1) * Q)
        scale = scale_ref[:, group * 2 * half : (group + 1) * 2 * half]
        for pair in range(half // 2):
            slot = first_slot + 2 * pair
            columns = [x_ref[block, spans[slot + part]] for part in range(2)]
            scaled = scaled_pair(columns, scale, slot)
            product = jnp.dot(tail_b, scaled, preferred_element_type=F32)
            for part in range(2):
                lane = slice(slot + part, slot + part + 1)
                index = 2 * pair + part
                state = product[:, part * P_SIZE : (part + 1) * P_SIZE] * final[:, lane]
                if group > 0:
                    state = state + state_ref[index, 0:N, :] * passing[:, lane]
                state_ref[index, 0:N, :] = state
    reach = stats_ref[16 + groups : 17 + groups, :]
    for index in range(half):
        lane = slice(first_slot + index, first_slot + index + 1)
        state_ref[index, N : N + 8, :] = jnp.broadcast_to(reach[:, lane], (8, P_SIZE))


def away_states_kernel(
    heads,
    groups,
    doc_hbm,
    rate_hbm,
    step_hbm,
    b_hbm,
    x_hbm,
    state_ref,
    stats_ref,
    scale_ref,
    tail_ref,
    logs_ref,
    x_ref,
    doc_ref,
    rate_ref,
    step_ref,
    b_ref,
    small_sems,
    wide_sems,
):
    half = heads // 2
    small = [
        pltpu.make_async_copy(src, dst, small_sems.at[i])
        for i, (src, dst) in enumerate(
            ((step_hbm, step_ref), (rate_hbm, rate_ref), (doc_hbm, doc_ref), (b_hbm, b_ref))
        )
    ]
    wide = [
        pltpu.make_async_copy(
            x_hbm.at[pl.ds(group * Q, Q), :],
            x_ref.at[pl.ds(group * Q, Q), :],
            wide_sems.at[group],
        )
        for group in range(groups)
    ]
    for copy in small + wide:
        copy.start()
    for copy in small:
        copy.wait()
    stats_ref[...] = jnp.zeros_like(stats_ref)
    base = lax.axis_index("seq") * (groups * Q)
    reach = jnp.ones((1, heads), F32)
    stats_ref[16:17, 0:heads] = reach
    step = stacked_groups(slot_rows(step_ref))
    logs = column_logs(step, rate_ref, heads)
    logs_ref[...] = logs
    scale_ref[...] = jnp.exp(-logs) * step.T
    finals = jnp.exp(logs[Q - 1 : Q, :])
    for group in range(groups):
        start = base + group * Q
        doc_first, next_end = group_bounds(doc_ref, start)
        final = finals[:, group * heads : (group + 1) * heads]
        passing = jnp.where(start + (Q - 1) < next_end, final, 0.0)
        positions = lax.broadcasted_iota(jnp.int32, (N, Q), 1) + start
        b_rows = b_ref[group * Q : (group + 1) * Q, :].astype(F32).T
        tail_ref[group] = jnp.where(positions >= doc_first, b_rows, 0.0).astype(BF16)
        reach = reach * passing
        stats_ref[group : group + 1, 0:heads] = final
        stats_ref[8 + group : 9 + group, 0:heads] = passing
        stats_ref[17 + group : 18 + group, 0:heads] = reach

    half_states(
        groups,
        half,
        x_ref,
        scale_ref,
        lambda group: tail_ref[group],
        stats_ref,
        state_ref,
        lambda group: wide[group].wait(),
    )


def own_states_kernel(heads, groups, stats_ref, scale_ref, tail_ref, x_ref, state_ref):
    half_states(
        groups,
        0,
        x_ref,
        scale_ref,
        lambda group: tail_ref[group],
        stats_ref,
        state_ref,
        lambda group: None,
    )


def half_inside(
    heads,
    groups,
    first_slot,
    skip_ref,
    stats_ref,
    scale_ref,
    tail_ref,
    decay_ref,
    masked_ref,
    x_ref,
    gate_ref,
    u_ref,
    v_ref,
    before_ref,
):
    half = heads // 2
    spans = head_spans(heads)
    skips = [skip_ref[head_of(first_slot + place, heads)] for place in range(half)]
    for group in range(groups):
        block = slice(group * Q, (group + 1) * Q)
        lanes = slice(group * heads, (group + 1) * heads)
        scale = scale_ref[:, lanes]
        decay = decay_ref[:, lanes]
        final = stats_ref[group : group + 1, :]
        passing = stats_ref[8 + group : 9 + group, :]
        masked = masked_ref[group]
        for pair in range(half // 2):
            slot = first_slot + 2 * pair
            columns = [x_ref[block, spans[slot + part]] for part in range(2)]
            scaled = scaled_pair(columns, scale, slot)
            product = jnp.dot(masked, scaled, preferred_element_type=F32)
            if group < groups - 1:
                states = jnp.dot(tail_ref[group], scaled, preferred_element_type=F32)
            for part in range(2):
                here = slice(part * P_SIZE, (part + 1) * P_SIZE)
                place = 2 * pair + part
                span = slice(place * P_SIZE, (place + 1) * P_SIZE)
                gate = 0.5 * gate_ref[block, spans[slot + part]].astype(F32)
                active = gate + gate * jnp.tanh(gate)
                carry = head_columns(decay, slot + part) * active
                direct = skips[place] * columns[part].astype(F32)
                u_ref[block, span] = product[:, here] * carry + direct * active
                v_ref[block, span] = carry
                if group < groups - 1:
                    lane = slice(slot + part, slot + part + 1)
                    state = states[:, here] * final[:, lane]
                    if group > 0:
                        state = state + before_ref[group - 1, place] * passing[:, lane]
                    before_ref[group, place] = state


def away_inside_kernel(
    heads,
    groups,
    doc_ref,
    skip_ref,
    logs_ref,
    b_ref,
    c_ref,
    stats_ref,
    scale_ref,
    tail_ref,
    x_ref,
    gate_ref,
    after_ref,
    u_ref,
    v_ref,
    before_ref,
    entry_c_ref,
    decay_ref,
    masked_ref,
    token_ref,
):
    base = lax.axis_index("seq") * (groups * Q)
    rows = lax.broadcasted_iota(jnp.int32, (Q, Q), 0)
    cols = lax.broadcasted_iota(jnp.int32, (Q, Q), 1)
    decay_ref[...] = jnp.exp(logs_ref[...])
    for group in range(groups):
        start = base + group * Q
        block = slice(group * Q, (group + 1) * Q)
        _, next_end = group_bounds(doc_ref, start)
        positions = lax.broadcasted_iota(jnp.int32, (Q, N), 0) + start
        entry_c = jnp.where(positions < next_end, c_ref[block, :].astype(F32), 0.0)
        entry_c_ref[block, :] = entry_c.astype(BF16)
        first = jnp.zeros((Q, Q), jnp.int32)
        end = jnp.int32(0)
        for k in range(doc_ref.shape[0]):
            end = end + doc_ref[k]
            first = jnp.where(end - start <= rows, end - start, first)
        scores = lax.dot_general(c_ref[block, :], b_ref[block, :], NT, preferred_element_type=F32)
        masked = jnp.where((cols <= rows) & (cols >= first), scores, 0.0)
        masked_ref[group] = masked.astype(BF16)
    half_inside(
        heads,
        groups,
        heads // 2,
        skip_ref,
        stats_ref,
        scale_ref,
        tail_ref,
        decay_ref,
        masked_ref,
        x_ref,
        gate_ref,
        u_ref,
        v_ref,
        before_ref,
    )
    token_ref[...] = jnp.zeros_like(token_ref)


def own_inside_kernel(
    heads,
    groups,
    skip_ref,
    stats_ref,
    scale_ref,
    tail_ref,
    decay_ref,
    masked_ref,
    x_ref,
    gate_ref,
    after_ref,
    u_ref,
    v_ref,
    before_ref,
    token_ref,
):
    half_inside(
        heads,
        groups,
        0,
        skip_ref,
        stats_ref,
        scale_ref,
        tail_ref,
        decay_ref,
        masked_ref,
        x_ref,
        gate_ref,
        u_ref,
        v_ref,
        before_ref,
    )
    token_ref[...] = jnp.zeros_like(token_ref)


def join_cores_kernel(
    own_ref, other_ref, step1_ref, step2_ref, step3_ref, step4_ref, here_ref, token_ref
):
    core = core_index()
    places = [(ref, part) for ref in (step1_ref, step2_ref, step3_ref) for part in range(2)]
    for slot, (joined_ref, part) in enumerate(places + [(step4_ref, 0), (here_ref, 0)]):
        own, other = own_ref[slot], other_ref[slot]
        earlier = jnp.where(core == 0, own, other)
        later = jnp.where(core == 0, other, own)
        later_pass = later[N : N + 1, :]
        joined_ref[part, 0:N, :] = later_pass * earlier[0:N, :] + later[0:N, :]
        joined_ref[part, N : N + 8, :] = later_pass * earlier[N : N + 8, :]
    token_ref[...] = jnp.zeros_like(token_ref)


def pack_kernel(step3_ref, step2_ref, step1_ref, step4_ref, last_ref, after_ref, packed_ref):
    for step, ref in enumerate((step1_ref, step2_ref, step3_ref)):
        packed_ref[2 * step] = ref[0]
        packed_ref[2 * step + 1] = ref[1]
    packed_ref[6] = step4_ref[0]
    packed_ref[7] = last_ref[0]


def row_total_kernel(packed_ref, swapped_ref, after_ref, total_ref, parts_ref):
    core = core_index()
    for ref, arrived_on in ((packed_ref, core), (swapped_ref, 1 - core)):
        for step in (1, 2, 3):
            chip = chip_at(1 - arrived_on, step)
            parts_ref[0, chip] = ref[2 * step - 2]
            parts_ref[1, chip] = ref[2 * step - 1]
        parts_ref[arrived_on, chip_at(core, 4)] = ref[6]
        parts_ref[arrived_on, chip_at(core, 0)] = ref[7]
    for which in range(2):
        total = parts_ref[which, 0, 0:N, :]
        for chip in range(1, Z_SIZE):
            total = parts_ref[which, chip, N : N + 1, :] * total + parts_ref[which, chip, 0:N, :]
        total_ref[which] = total


def entering_kernel(
    parts_ref,
    carried_ref,
    step1_ref,
    step2_ref,
    step3_ref,
    step4_ref,
    here_ref,
    token_ref,
    all_ref,
):
    row = lax.axis_index("seq") // (2 * Z_SIZE)
    core = core_index()
    for which in range(2):
        state = jnp.where(row > 0, carried_ref[which], 0.0)
        for chip in range(Z_SIZE):
            all_ref[which, chip] = state
            if chip < Z_SIZE - 1:
                state = parts_ref[which, chip, N : N + 1, :] * state + parts_ref[which, chip, 0:N, :]
    for step, pair_ref in ((1, step1_ref), (2, step2_ref), (3, step3_ref)):
        chip = chip_at(core, step)
        pair_ref[0] = all_ref[0, chip]
        pair_ref[1] = all_ref[1, chip]
    step4_ref[0] = all_ref[core, chip_at(core, 4)]
    here_ref[0] = all_ref[core, chip_at(core, 0)]
    here_ref[1] = all_ref[1 - core, chip_at(core, 0)]
    token_ref[...] = jnp.zeros_like(token_ref)


EARLY_SLOTS = (6, 7, 8, 9, 10, 11, 12, 13, 15)
LATE_SLOTS = (0, 1, 2, 3, 4, 5, 14)


def outputs_kernel(
    slots,
    half,
    groups,
    last,
    here_ref,
    arrived_ref,
    own_other_ref,
    away_other_ref,
    own_before_ref,
    away_before_ref,
    stats_ref,
    c_ref,
    own_u_ref,
    own_v_ref,
    away_u_ref,
    away_v_ref,
    sums_ref,
    gated_ref,
    squares_ref,
    first_ref,
):
    core = core_index()
    sides = (
        (own_other_ref, own_before_ref, own_u_ref, own_v_ref),
        (away_other_ref, away_before_ref, away_u_ref, away_v_ref),
    )
    for index, slot in enumerate(slots):
        side, place = slot // half, slot % half
        earlier_ref = sides[side][0]
        chip_state = here_ref[side] if place == half - 1 else arrived_ref[place]
        joined = earlier_ref[place, N : N + 1, :] * chip_state + earlier_ref[place, 0:N, :]
        first_ref[index] = jnp.where(core == 0, chip_state, joined)

    for group in range(groups):
        block = slice(group * Q, (group + 1) * Q)
        reach = stats_ref[16 + group : 17 + group, :]
        squares = sums_ref[block, :] if last else jnp.zeros((Q, P_SIZE), F32)
        for start in range(0, len(slots), 2):
            pair = range(start, min(start + 2, len(slots)))
            states = []
            for index in pair:
                side, place = slots[index] // half, slots[index] % half
                state = first_ref[index]
                if group > 0:
                    lane = slice(slots[index], slots[index] + 1)
                    state = state * reach[:, lane] + sides[side][1][group - 1, place]
                states.append(state.astype(BF16))
            both = jnp.concatenate(states, axis=1) if len(states) > 1 else states[0]
            carried = jnp.dot(c_ref[block, :], both, preferred_element_type=F32)
            for part, index in enumerate(pair):
                side, place = slots[index] // half, slots[index] % half
                _, _, u_ref, v_ref = sides[side]
                span = slice(place * P_SIZE, (place + 1) * P_SIZE)
                here = slice(part * P_SIZE, (part + 1) * P_SIZE)
                gated = u_ref[block, span] + v_ref[block, span] * carried[:, here]
                gated_ref[block, index * P_SIZE : (index + 1) * P_SIZE] = gated
                squares = squares + gated * gated
        if last:
            squares_ref[:, block] = jnp.broadcast_to(
                jnp.sum(squares.T, axis=0, keepdims=True), (8, Q)
            )
        else:
            squares_ref[block, :] = squares


def split_place(slot):
    early = slot in EARLY_SLOTS
    return (0, EARLY_SLOTS.index(slot)) if early else (1, LATE_SLOTS.index(slot))


def write_states_kernel(
    heads,
    groups,
    early_first_ref,
    late_first_ref,
    own_before_ref,
    away_before_ref,
    stats_ref,
    after_ref,
    states_hbm,
    token_ref,
    states_ref,
    sems,
):
    half = heads // 2
    copies = []
    places = [head_of(slot, heads) for slot in range(heads)]
    for group in range(groups):
        reach = stats_ref[16 + group : 17 + group, :]
        for side, before_ref in enumerate((own_before_ref, away_before_ref)):
            for index in range(half):
                slot = side * half + index
                which, at = split_place(slot)
                state = (early_first_ref, late_first_ref)[which][at]
                if group > 0:
                    state = state * reach[:, slot : slot + 1] + before_ref[group - 1, index]
                states_ref[group, slot] = state.T
                copy = pltpu.make_async_copy(
                    states_ref.at[group, slot],
                    states_hbm.at[group, places[slot]],
                    sems.at[group, slot],
                )
                copy.start()
                copies.append(copy)
    for copy in copies:
        copy.wait()
    token_ref[...] = jnp.zeros_like(token_ref)


SCALE_ROWS = 128


def scale_kernel(
    inner, heads, early_ref, late_ref, gain_ref, sum_ref, a_ref, b_ref, c_ref, after_ref, out_hbm, out_ref, sems
):
    mean = (sum_ref[...] + a_ref[...] + b_ref[...] + c_ref[...]) * (1.0 / inner)
    scale = lax.rsqrt(mean + 1e-05)
    half = heads // 2
    spans = head_spans(heads)
    copies = []
    for chunk in range(early_ref.shape[0] // SCALE_ROWS):
        block = slice(chunk * SCALE_ROWS, (chunk + 1) * SCALE_ROWS)
        column = jnp.broadcast_to(scale[0:1, block], (P_SIZE, SCALE_ROWS)).T
        for slot in range(heads):
            which, at = split_place(slot)
            gated_ref = (early_ref, late_ref)[which]
            span = slice(at * P_SIZE, (at + 1) * P_SIZE)
            place = spans[slot]
            out_ref[block, place] = (
                gated_ref[block, span] * column * gain_ref[:, place]
            ).astype(BF16)
        rows = pl.ds(chunk * SCALE_ROWS, SCALE_ROWS)
        copy = pltpu.make_async_copy(
            out_ref.at[rows, :], out_hbm.at[rows, :], sems.at[chunk]
        )
        copy.start()
        copies.append(copy)
    for copy in copies:
        copy.wait()


def cost(flops, bytes_accessed):
    return pl.CostEstimate(flops=flops, bytes_accessed=bytes_accessed, transcendentals=0)


def params(mebibytes):
    return pltpu.CompilerParams(vmem_limit_bytes=mebibytes * 1024 * 1024)


def local(
    head_input,
    gate_input,
    step_size,
    input_proj,
    output_proj,
    decay_rate,
    skip_gain,
    norm_gain,
    doc_lengths,
):
    row_count, width = head_input.shape
    heads = step_size.shape[1]
    half = heads // 2
    groups = row_count // Q
    sds = jax.ShapeDtypeStruct
    step_rows = step_size.T
    gain = norm_gain.reshape(1, width)
    smem = pl.BlockSpec(memory_space=pltpu.SMEM)
    vmem = pl.BlockSpec(memory_space=pltpu.VMEM)
    hbm = pl.BlockSpec(memory_space=pltpu.HBM)
    anywhere = pl.BlockSpec(memory_space=pl.ANY)
    dma = pltpu.SemaphoreType.DMA

    token = sds((8, P_SIZE), F32)
    half_state = sds((half, N + 8, P_SIZE), F32)
    half_before = sds((groups - 1, half, N, P_SIZE), F32)
    half_wide = sds((row_count, width // 2), F32)

    def in_hbm(*arrays):
        return [pltpu.with_memory_space_constraint(array, pltpu.HBM) for array in arrays]

    pair_state = sds((2, N + 8, P_SIZE), F32)
    one_state = sds((1, N + 8, P_SIZE), F32)
    pair_first = sds((2, N, P_SIZE), F32)
    one_first = sds((1, N, P_SIZE), F32)
    lanes = groups * heads

    away_state, stats, scale, tail, logs, input_copy = pl.pallas_call(
        functools.partial(away_states_kernel, heads, groups),
        in_specs=[hbm] * 5,
        out_specs=[vmem] * 6,
        out_shape=[
            half_state,
            sds((24, P_SIZE), F32),
            sds((Q, lanes), F32),
            sds((groups, N, Q), BF16),
            sds((Q, lanes), F32),
            sds((row_count, width), BF16),
        ],
        scratch_shapes=[
            pltpu.SMEM(doc_lengths.shape, jnp.int32),
            pltpu.SMEM(decay_rate.shape, F32),
            pltpu.VMEM((heads, row_count), F32),
            pltpu.VMEM((row_count, N), BF16),
            dma((4,)),
            dma((groups,)),
        ],
        compiler_params=params(16),
        cost_estimate=cost(200_000_000, 4_000_000),
        name="away_states",
    )(*in_hbm(doc_lengths, decay_rate, step_rows, input_proj, head_input))
    own_other = lax.ppermute(away_state, "seq", CORE_SWAP)

    own_state = pl.pallas_call(
        functools.partial(own_states_kernel, heads, groups),
        in_specs=[vmem] * 4,
        out_specs=vmem,
        out_shape=half_state,
        compiler_params=params(16),
        cost_estimate=cost(2_000_000_000, 4_000_000),
        name="own_states",
    )(stats, scale, tail, input_copy)

    *joined, joined_token = pl.pallas_call(
        join_cores_kernel,
        out_shape=[pair_state] * 3 + [one_state] * 2 + [token],
        compiler_params=params(8),
        cost_estimate=cost(1_000_000, 1_700_000),
        name="join_cores",
    )(own_state, own_other)
    here_part = joined.pop()
    arrived = [lax.ppermute(joined[k], "seq", AROUND[k]) for k in (2, 1, 0, 3)]
    arrived = [arrived[2], arrived[1], arrived[0], arrived[3]]
    away_other = lax.ppermute(own_state, "seq", CORE_SWAP)

    away_u, away_v, away_before, entry_c, decay, masked, away_token = pl.pallas_call(
        functools.partial(away_inside_kernel, heads, groups),
        in_specs=[smem] * 2 + [vmem] * 8 + [anywhere],
        out_specs=[vmem] * 7,
        out_shape=[half_wide] * 2
        + [
            half_before,
            sds((row_count, N), BF16),
            sds((Q, lanes), F32),
            sds((groups, Q, Q), BF16),
            token,
        ],
        compiler_params=params(24),
        cost_estimate=cost(8_000_000_000, 20_000_000),
        name="away_inside",
    )(
        doc_lengths,
        skip_gain,
        logs,
        input_proj,
        output_proj,
        stats,
        scale,
        tail,
        input_copy,
        gate_input,
        joined_token,
    )

    def pack(states, last, after, name):
        return pl.pallas_call(
            pack_kernel,
            in_specs=[vmem] * 5 + [anywhere],
            out_specs=vmem,
            out_shape=sds((8,) + last.shape[1:], F32),
            compiler_params=params(8),
            cost_estimate=cost(300_000, 1_100_000),
            name=name,
        )(*states[2::-1], states[3], last, after)

    packed_parts = pack(arrived, here_part, away_token, "pack_parts")
    swapped_parts = lax.ppermute(packed_parts, "seq", CORE_SWAP)
    total, parts = pl.pallas_call(
        row_total_kernel,
        in_specs=[vmem, vmem, anywhere],
        out_shape=[pair_first, sds((2, Z_SIZE, N + 8, P_SIZE), F32)],
        compiler_params=params(8),
        cost_estimate=cost(300_000, 600_000),
        name="row_total",
    )(packed_parts, swapped_parts, away_other)
    carried = lax.ppermute(total, "seq", NEXT_ROW)
    *steps, here, entering_token = pl.pallas_call(
        entering_kernel,
        out_shape=[pair_first] * 3 + [one_first, pair_first, token],
        scratch_shapes=[pltpu.VMEM((2, Z_SIZE, N, P_SIZE), F32)],
        compiler_params=params(8),
        cost_estimate=cost(1_000_000, 1_100_000),
        name="entering",
    )(parts, carried)
    returned = [lax.ppermute(steps[k], "seq", AROUND[k]) for k in (2, 1, 0, 3)]
    returned = [returned[2], returned[1], returned[0], returned[3]]

    own_u, own_v, own_before, own_token = pl.pallas_call(
        functools.partial(own_inside_kernel, heads, groups),
        in_specs=[smem] + [vmem] * 7 + [anywhere],
        out_specs=[vmem] * 4,
        out_shape=[half_wide] * 2 + [half_before, token],
        compiler_params=params(20),
        cost_estimate=cost(8_000_000_000, 20_000_000),
        name="own_inside",
    )(skip_gain, stats, scale, tail, decay, masked, input_copy, gate_input, entering_token)
    packed = pack(returned, here, own_token, "pack_states")
    swapped = lax.ppermute(packed, "seq", CORE_SWAP)

    def outputs(slots, last, arrived_states, sums):
        return pl.pallas_call(
            functools.partial(outputs_kernel, slots, half, groups, last),
            in_specs=[vmem] * 12 + [vmem if last else anywhere],
            out_specs=[vmem] * 3,
            out_shape=[
                sds((row_count, len(slots) * P_SIZE), F32),
                sds((8, row_count) if last else (row_count, P_SIZE), F32),
                sds((len(slots), N, P_SIZE), F32),
            ],
            compiler_params=params(26),
            cost_estimate=cost(2_000_000, 9_000),
            name="late_outputs" if last else "early_outputs",
        )(
            here,
            arrived_states,
            own_other,
            away_other,
            own_before,
            away_before,
            stats,
            entry_c,
            own_u,
            own_v,
            away_u,
            away_v,
            sums,
        )

    early_gated, early_sums, early_first = outputs(EARLY_SLOTS, False, packed, stats)
    late_gated, squares, late_first = outputs(LATE_SLOTS, True, swapped, early_sums)

    tp_size = 4
    sums = [
        lax.ppermute(squares, "tp", [(i, (i + k) % tp_size) for i in range(tp_size)])
        for k in range(1, tp_size)
    ]
    group_states, states_token = pl.pallas_call(
        functools.partial(write_states_kernel, heads, groups),
        in_specs=[vmem] * 5 + [anywhere],
        out_specs=[hbm, vmem],
        out_shape=[sds((groups, heads, P_SIZE, N), F32), token],
        scratch_shapes=[
            pltpu.VMEM((groups, heads, P_SIZE, N), F32),
            dma((groups, heads)),
        ],
        compiler_params=params(16),
        cost_estimate=cost(4_000_000_000, 9_000_000),
        name="write_states",
    )(early_first, late_first, own_before, away_before, stats, squares)
    mixed_out = pl.pallas_call(
        functools.partial(scale_kernel, width * tp_size, heads),
        in_specs=[vmem] * 7 + [anywhere],
        out_specs=hbm,
        out_shape=sds((row_count, width), BF16),
        scratch_shapes=[
            pltpu.VMEM((row_count, width), BF16),
            dma((row_count // SCALE_ROWS,)),
        ],
        compiler_params=params(16),
        cost_estimate=cost(5_000_000, 6_500_000),
        name="scale",
    )(early_gated, late_gated, gain, squares, *sums, states_token)
    return (mixed_out, group_states)


def solution(mesh):
    return jax.shard_map(
        local,
        mesh=mesh,
        in_specs=(
            P("seq", "tp"),
            P("seq", "tp"),
            P("seq", "tp"),
            P("seq", None),
            P("seq", None),
            P("tp"),
            P("tp"),
            P("tp"),
            P(),
        ),
        out_specs=(P("seq", "tp"), P("seq", "tp", None, None)),
        check_vma=False,
    )
```

```python
import functools
import jax
import jax.numpy as jnp
from jax import lax
from jax.experimental import pallas as pl
from jax.experimental.pallas import tpu as pltpu
from jax.sharding import PartitionSpec as P

P_SIZE = 128
N = 128
Q = 256
F32 = jnp.float32
BF16 = jnp.bfloat16
Y_SIZE = 4
Z_SIZE = 8
NT = (((1,), (1,)), ((), ()))


def seq_index(y, z, core):
    return ((y % Y_SIZE) * Z_SIZE + (z % Z_SIZE)) * 2 + core


def seq_pairs(move):
    pairs = []
    for y in range(Y_SIZE):
        for z in range(Z_SIZE):
            for core in range(2):
                pairs.append((seq_index(y, z, core), seq_index(*move(y, z, core))))
    return pairs


CORE_SWAP = seq_pairs(lambda y, z, core: (y, z, 1 - core))
NEXT_ROW = seq_pairs(lambda y, z, core: (y + 1, z, core))
AROUND = [
    seq_pairs(lambda y, z, core, step=step: (y, z + (step if core == 0 else -step), core))
    for step in range(1, 5)
]


def group_bounds(doc_ref, start):
    last = start + (Q - 1)
    doc_first = jnp.int32(0)
    next_end = jnp.int32(2147483647)
    end = jnp.int32(0)
    for k in range(doc_ref.shape[0]):
        end = end + doc_ref[k]
        doc_first = jnp.where(end <= last, end, doc_first)
        next_end = jnp.minimum(next_end, jnp.where(end >= start, end, 2147483647))
    return doc_first, next_end


def split3(values):
    high = values.astype(BF16)
    rest = values - high.astype(F32)
    mid = rest.astype(BF16)
    low = (rest - mid.astype(F32)).astype(BF16)
    return high, mid, low


def core_index():
    return lax.axis_index("seq") & 1


def ring_index():
    return (lax.axis_index("seq") // 2) & (Z_SIZE - 1)


def chip_at(core, step):
    return (ring_index() + jnp.where(core == 0, step, Z_SIZE - step)) & (Z_SIZE - 1)


def head_of(slot, heads):
    half = heads // 2
    core = core_index() if slot < half else 1 - core_index()
    place = slot % half
    if place < 6:
        return chip_at(core, place // 2 + 1) + half * (place % 2)
    return core * half + chip_at(core, 4 if place == 6 else 0)


def head_spans(heads):
    return [
        pl.ds(pl.multiple_of(head_of(slot, heads) * P_SIZE, P_SIZE), P_SIZE)
        for slot in range(heads)
    ]


def slot_rows(rows_ref):
    heads = rows_ref.shape[0]
    return jnp.concatenate(
        [rows_ref[pl.ds(head_of(slot, heads), 1), :] for slot in range(heads)], axis=0
    )


def stacked_groups(rows):
    groups = rows.shape[1] // Q
    return jnp.concatenate([rows[:, g * Q : (g + 1) * Q] for g in range(groups)], axis=0)


def column_logs(step, rate_ref, lower, heads):
    head_rows = lax.rem(lax.broadcasted_iota(jnp.int32, step.shape, 0), heads)
    rates = jnp.zeros_like(step)
    for slot in range(heads):
        rates = jnp.where(head_rows == slot, -rate_ref[head_of(slot, heads)], rates)
    return sum(
        lax.dot_general(lower, part, NT, preferred_element_type=F32)
        for part in split3(rates * step)
    )


def head_columns(values, head):
    return jnp.broadcast_to(values[:, head : head + 1], (values.shape[0], P_SIZE))


def scaled_pair(columns, scale, slot):
    parts = [
        (columns[part].astype(F32) * head_columns(scale, slot + part)).astype(BF16)
        for part in range(2)
    ]
    return jnp.concatenate(parts, axis=1)


def half_states(groups, first_slot, x_ref, scale_ref, tail_of, stats_ref, state_ref, ready):
    half = state_ref.shape[0]
    spans = head_spans(2 * half)
    for group in range(groups):
        final = stats_ref[group : group + 1, :]
        passing = stats_ref[8 + group : 9 + group, :]
        tail_b = tail_of(group)
        ready(group)
        block = slice(group * Q, (group + 1) * Q)
        scale = scale_ref[:, group * 2 * half : (group + 1) * 2 * half]
        for pair in range(half // 2):
            slot = first_slot + 2 * pair
            columns = [x_ref[block, spans[slot + part]] for part in range(2)]
            scaled = scaled_pair(columns, scale, slot)
            product = jnp.dot(tail_b, scaled, preferred_element_type=F32)
            for part in range(2):
                lane = slice(slot + part, slot + part + 1)
                index = 2 * pair + part
                state = product[:, part * P_SIZE : (part + 1) * P_SIZE] * final[:, lane]
                if group > 0:
                    state = state + state_ref[index, 0:N, :] * passing[:, lane]
                state_ref[index, 0:N, :] = state
    reach = stats_ref[16 + groups : 17 + groups, :]
    for index in range(half):
        lane = slice(first_slot + index, first_slot + index + 1)
        state_ref[index, N : N + 8, :] = jnp.broadcast_to(reach[:, lane], (8, P_SIZE))


def away_states_kernel(
    heads,
    groups,
    doc_hbm,
    rate_hbm,
    step_hbm,
    b_hbm,
    x_hbm,
    state_ref,
    stats_ref,
    scale_ref,
    tail_ref,
    logs_ref,
    x_ref,
    doc_ref,
    rate_ref,
    step_ref,
    b_ref,
    small_sems,
    wide_sems,
):
    half = heads // 2
    small = [
        pltpu.make_async_copy(src, dst, small_sems.at[i])
        for i, (src, dst) in enumerate(
            ((step_hbm, step_ref), (rate_hbm, rate_ref), (doc_hbm, doc_ref), (b_hbm, b_ref))
        )
    ]
    wide = [
        pltpu.make_async_copy(
            x_hbm.at[pl.ds(group * Q, Q), :],
            x_ref.at[pl.ds(group * Q, Q), :],
            wide_sems.at[group],
        )
        for group in range(groups)
    ]
    for copy in small + wide:
        copy.start()
    stats_ref[...] = jnp.zeros_like(stats_ref)
    rows = lax.broadcasted_iota(jnp.int32, (Q, Q), 0)
    cols = lax.broadcasted_iota(jnp.int32, (Q, Q), 1)
    lower = jnp.where(cols <= rows, 1.0, 0.0).astype(BF16)
    for copy in small[:2]:
        copy.wait()
    base = lax.axis_index("seq") * (groups * Q)
    reach = jnp.ones((1, heads), F32)
    stats_ref[16:17, 0:heads] = reach
    step = stacked_groups(slot_rows(step_ref))
    logs = column_logs(step, rate_ref, lower, heads)
    logs_ref[...] = logs
    scale_ref[...] = jnp.exp(-logs) * step.T
    finals = jnp.exp(logs[Q - 1 : Q, :])
    for copy in small[2:]:
        copy.wait()
    for group in range(groups):
        start = base + group * Q
        doc_first, next_end = group_bounds(doc_ref, start)
        final = finals[:, group * heads : (group + 1) * heads]
        passing = jnp.where(start + (Q - 1) < next_end, final, 0.0)
        positions = lax.broadcasted_iota(jnp.int32, (N, Q), 1) + start
        b_rows = b_ref[group * Q : (group + 1) * Q, :].astype(F32).T
        tail_ref[group] = jnp.where(positions >= doc_first, b_rows, 0.0).astype(BF16)
        reach = reach * passing
        stats_ref[group : group + 1, 0:heads] = final
        stats_ref[8 + group : 9 + group, 0:heads] = passing
        stats_ref[17 + group : 18 + group, 0:heads] = reach

    half_states(
        groups,
        half,
        x_ref,
        scale_ref,
        lambda group: tail_ref[group],
        stats_ref,
        state_ref,
        lambda group: wide[group].wait(),
    )


def own_states_kernel(heads, groups, stats_ref, scale_ref, tail_ref, x_ref, state_ref):
    half_states(
        groups,
        0,
        x_ref,
        scale_ref,
        lambda group: tail_ref[group],
        stats_ref,
        state_ref,
        lambda group: None,
    )


def half_inside(
    heads,
    groups,
    first_slot,
    skip_ref,
    stats_ref,
    scale_ref,
    tail_ref,
    decay_ref,
    masked_ref,
    x_ref,
    gate_ref,
    u_ref,
    v_ref,
    before_ref,
):
    half = heads // 2
    spans = head_spans(heads)
    skips = [skip_ref[head_of(first_slot + place, heads)] for place in range(half)]
    for group in range(groups):
        block = slice(group * Q, (group + 1) * Q)
        lanes = slice(group * heads, (group + 1) * heads)
        scale = scale_ref[:, lanes]
        decay = decay_ref[:, lanes]
        final = stats_ref[group : group + 1, :]
        passing = stats_ref[8 + group : 9 + group, :]
        masked = masked_ref[group]
        for pair in range(half // 2):
            slot = first_slot + 2 * pair
            columns = [x_ref[block, spans[slot + part]] for part in range(2)]
            scaled = scaled_pair(columns, scale, slot)
            product = jnp.dot(masked, scaled, preferred_element_type=F32)
            if group < groups - 1:
                states = jnp.dot(tail_ref[group], scaled, preferred_element_type=F32)
            for part in range(2):
                here = slice(part * P_SIZE, (part + 1) * P_SIZE)
                place = 2 * pair + part
                span = slice(place * P_SIZE, (place + 1) * P_SIZE)
                gate = 0.5 * gate_ref[block, spans[slot + part]].astype(F32)
                active = gate + gate * jnp.tanh(gate)
                carry = head_columns(decay, slot + part) * active
                direct = skips[place] * columns[part].astype(F32)
                u_ref[block, span] = product[:, here] * carry + direct * active
                v_ref[block, span] = carry
                if group < groups - 1:
                    lane = slice(slot + part, slot + part + 1)
                    state = states[:, here] * final[:, lane]
                    if group > 0:
                        state = state + before_ref[group - 1, place] * passing[:, lane]
                    before_ref[group, place] = state


def away_inside_kernel(
    heads,
    groups,
    doc_ref,
    skip_ref,
    logs_ref,
    b_ref,
    c_ref,
    stats_ref,
    scale_ref,
    tail_ref,
    x_ref,
    gate_ref,
    after_ref,
    u_ref,
    v_ref,
    before_ref,
    entry_c_ref,
    decay_ref,
    masked_ref,
    token_ref,
):
    base = lax.axis_index("seq") * (groups * Q)
    rows = lax.broadcasted_iota(jnp.int32, (Q, Q), 0)
    cols = lax.broadcasted_iota(jnp.int32, (Q, Q), 1)
    decay_ref[...] = jnp.exp(logs_ref[...])
    for group in range(groups):
        start = base + group * Q
        block = slice(group * Q, (group + 1) * Q)
        _, next_end = group_bounds(doc_ref, start)
        positions = lax.broadcasted_iota(jnp.int32, (Q, N), 0) + start
        entry_c = jnp.where(positions < next_end, c_ref[block, :].astype(F32), 0.0)
        entry_c_ref[block, :] = entry_c.astype(BF16)
        first = jnp.zeros((Q, Q), jnp.int32)
        end = jnp.int32(0)
        for k in range(doc_ref.shape[0]):
            end = end + doc_ref[k]
            first = jnp.where(end - start <= rows, end - start, first)
        scores = lax.dot_general(c_ref[block, :], b_ref[block, :], NT, preferred_element_type=F32)
        masked = jnp.where((cols <= rows) & (cols >= first), scores, 0.0)
        masked_ref[group] = masked.astype(BF16)
    half_inside(
        heads,
        groups,
        heads // 2,
        skip_ref,
        stats_ref,
        scale_ref,
        tail_ref,
        decay_ref,
        masked_ref,
        x_ref,
        gate_ref,
        u_ref,
        v_ref,
        before_ref,
    )
    token_ref[...] = jnp.zeros_like(token_ref)


def own_inside_kernel(
    heads,
    groups,
    skip_ref,
    stats_ref,
    scale_ref,
    tail_ref,
    decay_ref,
    masked_ref,
    x_ref,
    gate_ref,
    after_ref,
    u_ref,
    v_ref,
    before_ref,
    token_ref,
):
    half_inside(
        heads,
        groups,
        0,
        skip_ref,
        stats_ref,
        scale_ref,
        tail_ref,
        decay_ref,
        masked_ref,
        x_ref,
        gate_ref,
        u_ref,
        v_ref,
        before_ref,
    )
    token_ref[...] = jnp.zeros_like(token_ref)


def join_cores_kernel(
    own_ref, other_ref, step1_ref, step2_ref, step3_ref, step4_ref, here_ref, token_ref
):
    core = core_index()
    places = [(ref, part) for ref in (step1_ref, step2_ref, step3_ref) for part in range(2)]
    for slot, (joined_ref, part) in enumerate(places + [(step4_ref, 0), (here_ref, 0)]):
        own, other = own_ref[slot], other_ref[slot]
        earlier = jnp.where(core == 0, own, other)
        later = jnp.where(core == 0, other, own)
        later_pass = later[N : N + 1, :]
        joined_ref[part, 0:N, :] = later_pass * earlier[0:N, :] + later[0:N, :]
        joined_ref[part, N : N + 8, :] = later_pass * earlier[N : N + 8, :]
    token_ref[...] = jnp.zeros_like(token_ref)


def pack_kernel(step3_ref, step2_ref, step1_ref, step4_ref, last_ref, after_ref, packed_ref):
    for step, ref in enumerate((step1_ref, step2_ref, step3_ref)):
        packed_ref[2 * step] = ref[0]
        packed_ref[2 * step + 1] = ref[1]
    packed_ref[6] = step4_ref[0]
    packed_ref[7] = last_ref[0]


def row_total_kernel(packed_ref, swapped_ref, after_ref, total_ref, parts_ref):
    core = core_index()
    for ref, arrived_on in ((packed_ref, core), (swapped_ref, 1 - core)):
        for step in (1, 2, 3):
            chip = chip_at(1 - arrived_on, step)
            parts_ref[0, chip] = ref[2 * step - 2]
            parts_ref[1, chip] = ref[2 * step - 1]
        parts_ref[arrived_on, chip_at(core, 4)] = ref[6]
        parts_ref[arrived_on, chip_at(core, 0)] = ref[7]
    for which in range(2):
        total = parts_ref[which, 0, 0:N, :]
        for chip in range(1, Z_SIZE):
            total = parts_ref[which, chip, N : N + 1, :] * total + parts_ref[which, chip, 0:N, :]
        total_ref[which] = total


def entering_kernel(
    parts_ref,
    carried_ref,
    step1_ref,
    step2_ref,
    step3_ref,
    step4_ref,
    here_ref,
    token_ref,
    all_ref,
):
    row = lax.axis_index("seq") // (2 * Z_SIZE)
    core = core_index()
    for which in range(2):
        state = jnp.where(row > 0, carried_ref[which], 0.0)
        for chip in range(Z_SIZE):
            all_ref[which, chip] = state
            if chip < Z_SIZE - 1:
                state = parts_ref[which, chip, N : N + 1, :] * state + parts_ref[which, chip, 0:N, :]
    for step, pair_ref in ((1, step1_ref), (2, step2_ref), (3, step3_ref)):
        chip = chip_at(core, step)
        pair_ref[0] = all_ref[0, chip]
        pair_ref[1] = all_ref[1, chip]
    step4_ref[0] = all_ref[core, chip_at(core, 4)]
    here_ref[0] = all_ref[core, chip_at(core, 0)]
    here_ref[1] = all_ref[1 - core, chip_at(core, 0)]
    token_ref[...] = jnp.zeros_like(token_ref)


EARLY_SLOTS = (6, 7, 8, 9, 10, 11, 12, 13, 15)
LATE_SLOTS = (0, 1, 2, 3, 4, 5, 14)


def outputs_kernel(
    slots,
    half,
    groups,
    last,
    here_ref,
    arrived_ref,
    own_other_ref,
    away_other_ref,
    own_before_ref,
    away_before_ref,
    stats_ref,
    c_ref,
    own_u_ref,
    own_v_ref,
    away_u_ref,
    away_v_ref,
    sums_ref,
    gated_ref,
    squares_ref,
    first_ref,
):
    core = core_index()
    sides = (
        (own_other_ref, own_before_ref, own_u_ref, own_v_ref),
        (away_other_ref, away_before_ref, away_u_ref, away_v_ref),
    )
    for index, slot in enumerate(slots):
        side, place = slot // half, slot % half
        earlier_ref = sides[side][0]
        chip_state = here_ref[side] if place == half - 1 else arrived_ref[place]
        joined = earlier_ref[place, N : N + 1, :] * chip_state + earlier_ref[place, 0:N, :]
        first_ref[index] = jnp.where(core == 0, chip_state, joined)

    for group in range(groups):
        block = slice(group * Q, (group + 1) * Q)
        reach = stats_ref[16 + group : 17 + group, :]
        squares = sums_ref[block, :] if last else jnp.zeros((Q, P_SIZE), F32)
        for start in range(0, len(slots), 2):
            pair = range(start, min(start + 2, len(slots)))
            states = []
            for index in pair:
                side, place = slots[index] // half, slots[index] % half
                state = first_ref[index]
                if group > 0:
                    lane = slice(slots[index], slots[index] + 1)
                    state = state * reach[:, lane] + sides[side][1][group - 1, place]
                states.append(state.astype(BF16))
            both = jnp.concatenate(states, axis=1) if len(states) > 1 else states[0]
            carried = jnp.dot(c_ref[block, :], both, preferred_element_type=F32)
            for part, index in enumerate(pair):
                side, place = slots[index] // half, slots[index] % half
                _, _, u_ref, v_ref = sides[side]
                span = slice(place * P_SIZE, (place + 1) * P_SIZE)
                here = slice(part * P_SIZE, (part + 1) * P_SIZE)
                gated = u_ref[block, span] + v_ref[block, span] * carried[:, here]
                gated_ref[block, index * P_SIZE : (index + 1) * P_SIZE] = gated
                squares = squares + gated * gated
        if last:
            squares_ref[:, block] = jnp.broadcast_to(
                jnp.sum(squares.T, axis=0, keepdims=True), (8, Q)
            )
        else:
            squares_ref[block, :] = squares


def split_place(slot):
    early = slot in EARLY_SLOTS
    return (0, EARLY_SLOTS.index(slot)) if early else (1, LATE_SLOTS.index(slot))


def write_states_kernel(
    heads,
    groups,
    early_first_ref,
    late_first_ref,
    own_before_ref,
    away_before_ref,
    stats_ref,
    after_ref,
    states_hbm,
    token_ref,
    states_ref,
    sems,
):
    half = heads // 2
    copies = []
    places = [head_of(slot, heads) for slot in range(heads)]
    for group in range(groups):
        reach = stats_ref[16 + group : 17 + group, :]
        for side, before_ref in enumerate((own_before_ref, away_before_ref)):
            for index in range(half):
                slot = side * half + index
                which, at = split_place(slot)
                state = (early_first_ref, late_first_ref)[which][at]
                if group > 0:
                    state = state * reach[:, slot : slot + 1] + before_ref[group - 1, index]
                states_ref[group, slot] = state.T
                copy = pltpu.make_async_copy(
                    states_ref.at[group, slot],
                    states_hbm.at[group, places[slot]],
                    sems.at[group, slot],
                )
                copy.start()
                copies.append(copy)
    for copy in copies:
        copy.wait()
    token_ref[...] = jnp.zeros_like(token_ref)


SCALE_ROWS = 128


def scale_kernel(
    inner, heads, early_ref, late_ref, gain_ref, sum_ref, a_ref, b_ref, c_ref, after_ref, out_hbm, out_ref, sems
):
    mean = (sum_ref[...] + a_ref[...] + b_ref[...] + c_ref[...]) * (1.0 / inner)
    scale = lax.rsqrt(mean + 1e-05)
    half = heads // 2
    spans = head_spans(heads)
    copies = []
    for chunk in range(early_ref.shape[0] // SCALE_ROWS):
        block = slice(chunk * SCALE_ROWS, (chunk + 1) * SCALE_ROWS)
        column = jnp.broadcast_to(scale[0:1, block], (P_SIZE, SCALE_ROWS)).T
        for slot in range(heads):
            which, at = split_place(slot)
            gated_ref = (early_ref, late_ref)[which]
            span = slice(at * P_SIZE, (at + 1) * P_SIZE)
            place = spans[slot]
            out_ref[block, place] = (
                gated_ref[block, span] * column * gain_ref[:, place]
            ).astype(BF16)
        rows = pl.ds(chunk * SCALE_ROWS, SCALE_ROWS)
        copy = pltpu.make_async_copy(
            out_ref.at[rows, :], out_hbm.at[rows, :], sems.at[chunk]
        )
        copy.start()
        copies.append(copy)
    for copy in copies:
        copy.wait()


def cost(flops, bytes_accessed):
    return pl.CostEstimate(flops=flops, bytes_accessed=bytes_accessed, transcendentals=0)


def params(mebibytes):
    return pltpu.CompilerParams(vmem_limit_bytes=mebibytes * 1024 * 1024)


def local(
    head_input,
    gate_input,
    step_size,
    input_proj,
    output_proj,
    decay_rate,
    skip_gain,
    norm_gain,
    doc_lengths,
):
    row_count, width = head_input.shape
    heads = step_size.shape[1]
    half = heads // 2
    groups = row_count // Q
    sds = jax.ShapeDtypeStruct
    step_rows = step_size.T
    gain = norm_gain.reshape(1, width)
    smem = pl.BlockSpec(memory_space=pltpu.SMEM)
    vmem = pl.BlockSpec(memory_space=pltpu.VMEM)
    hbm = pl.BlockSpec(memory_space=pltpu.HBM)
    anywhere = pl.BlockSpec(memory_space=pl.ANY)
    dma = pltpu.SemaphoreType.DMA

    token = sds((8, P_SIZE), F32)
    half_state = sds((half, N + 8, P_SIZE), F32)
    half_before = sds((groups - 1, half, N, P_SIZE), F32)
    half_wide = sds((row_count, width // 2), F32)

    def in_hbm(*arrays):
        return [pltpu.with_memory_space_constraint(array, pltpu.HBM) for array in arrays]

    pair_state = sds((2, N + 8, P_SIZE), F32)
    one_state = sds((1, N + 8, P_SIZE), F32)
    pair_first = sds((2, N, P_SIZE), F32)
    one_first = sds((1, N, P_SIZE), F32)
    lanes = groups * heads

    away_state, stats, scale, tail, logs, input_copy = pl.pallas_call(
        functools.partial(away_states_kernel, heads, groups),
        in_specs=[hbm] * 5,
        out_specs=[vmem] * 6,
        out_shape=[
            half_state,
            sds((24, P_SIZE), F32),
            sds((Q, lanes), F32),
            sds((groups, N, Q), BF16),
            sds((Q, lanes), F32),
            sds((row_count, width), BF16),
        ],
        scratch_shapes=[
            pltpu.SMEM(doc_lengths.shape, jnp.int32),
            pltpu.SMEM(decay_rate.shape, F32),
            pltpu.VMEM((heads, row_count), F32),
            pltpu.VMEM((row_count, N), BF16),
            dma((4,)),
            dma((groups,)),
        ],
        compiler_params=params(16),
        cost_estimate=cost(200_000_000, 4_000_000),
        name="away_states",
    )(*in_hbm(doc_lengths, decay_rate, step_rows, input_proj, head_input))
    own_other = lax.ppermute(away_state, "seq", CORE_SWAP)

    own_state = pl.pallas_call(
        functools.partial(own_states_kernel, heads, groups),
        in_specs=[vmem] * 4,
        out_specs=vmem,
        out_shape=half_state,
        compiler_params=params(16),
        cost_estimate=cost(2_000_000_000, 4_000_000),
        name="own_states",
    )(stats, scale, tail, input_copy)

    *joined, joined_token = pl.pallas_call(
        join_cores_kernel,
        out_shape=[pair_state] * 3 + [one_state] * 2 + [token],
        compiler_params=params(8),
        cost_estimate=cost(1_000_000, 1_700_000),
        name="join_cores",
    )(own_state, own_other)
    here_part = joined.pop()
    arrived = [lax.ppermute(joined[k], "seq", AROUND[k]) for k in (2, 1, 0, 3)]
    arrived = [arrived[2], arrived[1], arrived[0], arrived[3]]
    away_other = lax.ppermute(own_state, "seq", CORE_SWAP)

    away_u, away_v, away_before, entry_c, decay, masked, away_token = pl.pallas_call(
        functools.partial(away_inside_kernel, heads, groups),
        in_specs=[smem] * 2 + [vmem] * 8 + [anywhere],
        out_specs=[vmem] * 7,
        out_shape=[half_wide] * 2
        + [
            half_before,
            sds((row_count, N), BF16),
            sds((Q, lanes), F32),
            sds((groups, Q, Q), BF16),
            token,
        ],
        compiler_params=params(24),
        cost_estimate=cost(8_000_000_000, 20_000_000),
        name="away_inside",
    )(
        doc_lengths,
        skip_gain,
        logs,
        input_proj,
        output_proj,
        stats,
        scale,
        tail,
        input_copy,
        gate_input,
        joined_token,
    )

    def pack(states, last, after, name):
        return pl.pallas_call(
            pack_kernel,
            in_specs=[vmem] * 5 + [anywhere],
            out_specs=vmem,
            out_shape=sds((8,) + last.shape[1:], F32),
            compiler_params=params(8),
            cost_estimate=cost(300_000, 1_100_000),
            name=name,
        )(*states[2::-1], states[3], last, after)

    packed_parts = pack(arrived, here_part, away_token, "pack_parts")
    swapped_parts = lax.ppermute(packed_parts, "seq", CORE_SWAP)
    total, parts = pl.pallas_call(
        row_total_kernel,
        in_specs=[vmem, vmem, anywhere],
        out_shape=[pair_first, sds((2, Z_SIZE, N + 8, P_SIZE), F32)],
        compiler_params=params(8),
        cost_estimate=cost(300_000, 600_000),
        name="row_total",
    )(packed_parts, swapped_parts, away_other)
    carried = lax.ppermute(total, "seq", NEXT_ROW)
    *steps, here, entering_token = pl.pallas_call(
        entering_kernel,
        out_shape=[pair_first] * 3 + [one_first, pair_first, token],
        scratch_shapes=[pltpu.VMEM((2, Z_SIZE, N, P_SIZE), F32)],
        compiler_params=params(8),
        cost_estimate=cost(1_000_000, 1_100_000),
        name="entering",
    )(parts, carried)
    returned = [lax.ppermute(steps[k], "seq", AROUND[k]) for k in (2, 1, 0, 3)]
    returned = [returned[2], returned[1], returned[0], returned[3]]

    own_u, own_v, own_before, own_token = pl.pallas_call(
        functools.partial(own_inside_kernel, heads, groups),
        in_specs=[smem] + [vmem] * 7 + [anywhere],
        out_specs=[vmem] * 4,
        out_shape=[half_wide] * 2 + [half_before, token],
        compiler_params=params(20),
        cost_estimate=cost(8_000_000_000, 20_000_000),
        name="own_inside",
    )(skip_gain, stats, scale, tail, decay, masked, input_copy, gate_input, entering_token)
    packed = pack(returned, here, own_token, "pack_states")
    swapped = lax.ppermute(packed, "seq", CORE_SWAP)

    def outputs(slots, last, arrived_states, sums):
        return pl.pallas_call(
            functools.partial(outputs_kernel, slots, half, groups, last),
            in_specs=[vmem] * 12 + [vmem if last else anywhere],
            out_specs=[vmem] * 3,
            out_shape=[
                sds((row_count, len(slots) * P_SIZE), F32),
                sds((8, row_count) if last else (row_count, P_SIZE), F32),
                sds((len(slots), N, P_SIZE), F32),
            ],
            compiler_params=params(26),
            cost_estimate=cost(2_000_000, 9_000),
            name="late_outputs" if last else "early_outputs",
        )(
            here,
            arrived_states,
            own_other,
            away_other,
            own_before,
            away_before,
            stats,
            entry_c,
            own_u,
            own_v,
            away_u,
            away_v,
            sums,
        )

    early_gated, early_sums, early_first = outputs(EARLY_SLOTS, False, packed, stats)
    late_gated, squares, late_first = outputs(LATE_SLOTS, True, swapped, early_sums)

    tp_size = 4
    sums = [
        lax.ppermute(squares, "tp", [(i, (i + k) % tp_size) for i in range(tp_size)])
        for k in range(1, tp_size)
    ]
    group_states, states_token = pl.pallas_call(
        functools.partial(write_states_kernel, heads, groups),
        in_specs=[vmem] * 5 + [anywhere],
        out_specs=[hbm, vmem],
        out_shape=[sds((groups, heads, P_SIZE, N), F32), token],
        scratch_shapes=[
            pltpu.VMEM((groups, heads, P_SIZE, N), F32),
            dma((groups, heads)),
        ],
        compiler_params=params(16),
        cost_estimate=cost(4_000_000_000, 9_000_000),
        name="write_states",
    )(early_first, late_first, own_before, away_before, stats, squares)
    mixed_out = pl.pallas_call(
        functools.partial(scale_kernel, width * tp_size, heads),
        in_specs=[vmem] * 7 + [anywhere],
        out_specs=hbm,
        out_shape=sds((row_count, width), BF16),
        scratch_shapes=[
            pltpu.VMEM((row_count, width), BF16),
            dma((row_count // SCALE_ROWS,)),
        ],
        compiler_params=params(16),
        cost_estimate=cost(5_000_000, 6_500_000),
        name="scale",
    )(early_gated, late_gated, gain, squares, *sums, states_token)
    return (mixed_out, group_states)


def solution(mesh):
    return jax.shard_map(
        local,
        mesh=mesh,
        in_specs=(
            P("seq", "tp"),
            P("seq", "tp"),
            P("seq", "tp"),
            P("seq", None),
            P("seq", None),
            P("tp"),
            P("tp"),
            P("tp"),
            P(),
        ),
        out_specs=(P("seq", "tp"), P("seq", "tp", None, None)),
        check_vma=False,
    )
```
